128 devices in a mesh: chan: 8 (over y, x_hi), space: 16 (over z, x_lo, core).
Axes of the slice: x: 4 (x_hi: 2, x_lo: 2; x = x_hi * 2 + x_lo), y: 4, z: 4, core: 2. Of those that a mesh axis runs over, the one named last changes fastest.
Arguments:
- volume: bfloat16 [64, 16, 256, 128], P('space', None, 'chan'), may hold values from -6 to 6
- kernel: bfloat16 [27, 256, 256], P(None, 'chan'), may hold values from -0.078125 to 0.078125
- bias: float32 [256], P('chan'), may hold values from -3 to 3
- cotangent: bfloat16 [64, 16, 256, 128], P('space', None, 'chan'), may hold values from -6 to 6
Outputs:
- output: bfloat16 [64, 16, 256, 128], P('space', None, 'chan')
- input_grad: bfloat16 [64, 16, 256, 128], P('space', None, 'chan')
- weight_grad: float32 [27, 256, 256], P(None, 'chan')
The draws below stay inside these ranges and needn't reach their ends.
All inputs are finite; a program needn't handle non-finite values.
Results may differ from the reference program's by a relative error of at most 0.0049.
Values may be sent and summed in bfloat16 or wider, within the bound.
No kernel may reach another device: no remote copies, remote signals or barrier semaphores. Data moves between devices by JAX's collectives and lax.ppermute only.
A program may use at most 128 MiB of HBM per device.

```python
import math
import jax
import jax.numpy as jnp
from jax import lax

CIN = 256
COUT = 256
TAPS = 27
NX = 64
NY = 16
NZ = 128


def block_scale(own_key, extent, shards, least, largest):
    gain, own = 1.0, jax.random.fold_in(own_key, 6)
    for dim, blocks in shards:
        draws = jnp.exp(jax.random.uniform(jax.random.fold_in(own, dim), (blocks,), jnp.float32, least / len(shards), largest / len(shards)))
        gain = gain * jnp.repeat(draws, extent[dim] // blocks).reshape([-1 if axis == dim else 1 for axis in range(len(extent))])
    return gain


def noise(stream_key, extent, width, bound, shards=(), held_as=jnp.bfloat16):
    drawn = width * jax.random.normal(stream_key, extent, jnp.float32)
    if shards:
        drawn = drawn * block_scale(stream_key, extent, shards, -0.22, 0.18)
    return jnp.clip(drawn, -bound, bound).astype(held_as)


def setup_inputs(seed: int = 0) -> dict:
    streams_of = jax.random.split(jax.random.key(seed), 5)
    return {
        "volume": noise(streams_of[0], (NX, NY, CIN, NZ), 1.0, 6.0, ((0, 16), (2, 8))),
        "kernel": noise(streams_of[1], (TAPS, COUT, CIN), (TAPS * CIN) ** -0.5, 0.078125, ((1, 8),)),
        "bias": noise(streams_of[2], (COUT,), 0.5, 3.0, ((0, 8),), jnp.float32),
        "cotangent": noise(streams_of[3], (NX, NY, COUT, NZ), 1.0, 6.0, ((0, 16), (2, 8))),
    }


def tap_list():
    return [(first, second, third) for first in range(3) for second in range(3) for third in range(3)]

def reference(volume, kernel, bias, cotangent):
    volume_last = jnp.transpose(volume, (0, 1, 3, 2))
    cotangent_last = jnp.transpose(cotangent, (0, 1, 3, 2))
    size_x, size_y, size_z, chans_in = volume_last.shape
    chans_out = kernel.shape[1]
    cells = size_x * size_y * size_z
    kernel_f = jnp.transpose(kernel.astype(jnp.float32), (0, 2, 1))
    padded = jnp.pad(volume_last.astype(jnp.float32), ((1, 1), (1, 1), (1, 1), (0, 0)))
    accum = jnp.zeros((cells, chans_out), jnp.float32)
    for index_tap, (first, second, third) in enumerate(tap_list()):
        slab = padded[first:first + size_x, second:second + size_y, third:third + size_z, :].reshape(cells, chans_in)
        accum = accum + jnp.dot(slab, kernel_f[index_tap], precision=lax.Precision.HIGHEST, preferred_element_type=jnp.float32)
    pre = accum + bias.astype(jnp.float32)
    sigmoid_pre = jax.nn.sigmoid(pre)
    output = (pre * sigmoid_pre).astype(jnp.bfloat16).reshape(size_x, size_y, size_z, chans_out)
    grad_pre = (cotangent_last.reshape(cells, chans_out).astype(jnp.float32) * sigmoid_pre * (1.0 + pre * (1.0 - sigmoid_pre))).astype(jnp.bfloat16)
    grad_f = grad_pre.astype(jnp.float32)
    parts = []
    for index_tap, (first, second, third) in enumerate(tap_list()):
        slab = padded[first:first + size_x, second:second + size_y, third:third + size_z, :].reshape(cells, chans_in)
        parts.append(jnp.dot(grad_f.T, slab, precision=lax.Precision.HIGHEST, preferred_element_type=jnp.float32))
    weight_grad = jnp.stack(parts) / math.sqrt(cells)
    grad_padded = jnp.pad(grad_f.reshape(size_x, size_y, size_z, chans_out), ((1, 1), (1, 1), (1, 1), (0, 0)))
    back = jnp.zeros((cells, chans_in), jnp.float32)
    for index_tap, (first, second, third) in enumerate(tap_list()):
        slab = grad_padded[2 - first:2 - first + size_x, 2 - second:2 - second + size_y, 2 - third:2 - third + size_z, :].reshape(cells, chans_out)
        back = back + jnp.dot(slab, kernel_f[index_tap].T, precision=lax.Precision.HIGHEST, preferred_element_type=jnp.float32)
    input_grad = back.astype(jnp.bfloat16).reshape(size_x, size_y, size_z, chans_in)
    return (jnp.transpose(output, (0, 1, 3, 2)), jnp.transpose(input_grad, (0, 1, 3, 2)), weight_grad)
```

```python
import functools
import math

import jax
import jax.numpy as jnp
from jax import lax
from jax.experimental import pallas as pl
from jax.experimental.pallas import tpu as pltpu
from jax.sharding import PartitionSpec as P

BF16 = jnp.bfloat16
F32 = jnp.float32
VMEM_LIMIT = 44 * 1024 * 1024


def moved(value, step):
    if step == 0:
        return value
    size = value.shape[-1]
    lane = lax.broadcasted_iota(jnp.int32, value.shape, value.ndim - 1)
    rolled = pltpu.roll(value, step % size, value.ndim - 1)
    edge = 0 if step == 1 else size - 1
    return jnp.where(lane == edge, 0.0, rolled)


def pair_of(ref, plane, row):
    return jnp.concatenate([ref[plane, row], ref[plane, row + 1]], axis=1)


def forward_body(at, own, left, right, far_lo, far_hi, kernel, bias, cot_own, cot_other,
                 out_own, out_other, grad, field):
    here_y, half = at[0], at[1]
    planes, rows = own.shape[0], own.shape[1]
    lines = own.shape[2]
    split = far_lo.shape[0]

    def fill(plane, carry):
        field[plane, 9 * half] = jnp.zeros(field.shape[2:], BF16)
        for row in range(rows):
            for shift, ref in ((0, own), (3, left), (1, right)):
                start = pl.multiple_of(lax.rem(here_y + shift, 4) * lines, lines)
                field[plane, row + 1 - half, pl.ds(start, lines), :] = ref[plane, row]
        return carry

    lax.fori_loop(0, planes, fill, 0)
    start = pl.multiple_of(lax.rem(here_y + 2, 4) * lines, lines)

    def fill_far(plane, carry):
        for row in range(rows):
            field[plane, row + 1 - half, pl.ds(start, lines), :] = far_lo[plane, row]
            field[plane + split, row + 1 - half, pl.ds(start, lines), :] = far_hi[plane, row]
        return carry

    lax.fori_loop(0, split, fill_far, 0)
    outs = kernel.shape[1] // 3
    half_outs = outs // 2

    def step(index, carry):
        plane, row = index // 4, 2 * lax.rem(index, 4)
        total = jnp.zeros((3 * outs, 256), F32)
        for a in range(3):
            for b in range(3):
                total = total + jnp.dot(
                    kernel[3 * a + b], pair_of(field, plane + a, row + b),
                    preferred_element_type=F32,
                )
        for r in range(2):
            part = total[:, 128 * r : 128 * r + 128]
            pre = (
                moved(part[:outs], 1) + part[outs : 2 * outs] + moved(part[2 * outs :], -1)
                + bias[...]
            )
            sig = 1.0 / (1.0 + jnp.exp(-pre))
            out = (pre * sig).astype(BF16)
            out_own[plane, row + r] = out[:half_outs]
            out_other[plane, row + r] = out[half_outs:]
            cot = jnp.concatenate(
                [cot_own[plane, row + r], cot_other[plane, row + r]], axis=0
            ).astype(F32)
            grad[plane, row + r] = (cot * sig * (1.0 + pre * (1.0 - sig))).astype(BF16)
        return carry

    lax.fori_loop(0, 16, step, 0)


def spread(line):
    wide = line.astype(F32)
    return [moved(wide, c - 1).astype(BF16) for c in range(3)]


def weight_body(at, field, grad, sums, stacked):
    core = at[2]
    planes, rows, outs = grad.shape[0], grad.shape[1], grad.shape[2]

    def fill(plane, carry):
        for row in range(rows):
            for c, line in enumerate(spread(grad[plane, row])):
                stacked[plane, row, outs * c : outs * (c + 1), :] = line
        return carry

    lax.fori_loop(0, planes, fill, 0)

    def step(tap, carry):
        a, b = tap // 3, lax.rem(tap, 3)
        total = jnp.zeros((3 * outs, 256), F32)
        for plane in range(planes):
            grads = jnp.concatenate([stacked[plane, row] for row in range(rows)], axis=1)
            cells = jnp.concatenate([field[plane + a, row + b] for row in range(rows)], axis=1)
            total = total + lax.dot_general(
                grads, cells, (((1,), (1,)), ((), ())), preferred_element_type=F32
            )
        for c in range(3):
            for side in range(2):
                for part in range(2):
                    low = outs * c + 32 * side + 16 * part
                    sums[part ^ core, side, 3 * tap + c] = total[low : low + 16]
        return carry

    lax.fori_loop(0, 9, step, 0)


def input_body(at, grad, edge, low, high, turned, own, parts, stacked, held):
    here_y, half = at[0], at[1]
    planes, rows, outs = grad.shape[0], grad.shape[1], grad.shape[2]

    def put(plane, row, line):
        for c, value in enumerate(spread(line)):
            stacked[plane, row, outs * c : outs * (c + 1), :] = value

    beside = 9 * (1 - half)

    def fill(plane, carry):
        for row in range(rows):
            put(plane + 1, row + 1, grad[plane, row])
        put(plane + 1, beside, edge[plane])
        return carry

    lax.fori_loop(0, planes, fill, 0)
    for row in range(rows):
        put(0, row + 1, low[row])
        put(planes + 1, row + 1, high[row])
    put(0, beside, low[rows])
    put(planes + 1, beside, high[rows])
    for plane in range(planes + 2):
        stacked[plane, 9 * half] = jnp.zeros(stacked.shape[2:], BF16)

    def step(index, carry):
        plane, row = index // 4, 2 * lax.rem(index, 4)
        terms = jnp.concatenate(
            [
                pair_of(stacked, plane + 2 - a, row + 2 - b)
                for a in range(3)
                for b in range(3)
            ],
            axis=0,
        )
        total = jnp.dot(turned[...], terms, preferred_element_type=F32)
        held[...] = total
        mine = held[pl.ds(pl.multiple_of(64 * here_y, 64), 64), :]
        for r in range(2):
            own[plane, row + r] = mine[:, 128 * r : 128 * r + 128]
            for j in range(4):
                parts[lax.rem(j + 4 - here_y, 4), plane, row + r] = total[
                    64 * j : 64 * j + 64, 128 * r : 128 * r + 128
                ].astype(BF16)
        return carry

    lax.fori_loop(0, 16, step, 0)


def call(body, n_in, outs, scratch, flops):
    vmem = pl.BlockSpec(memory_space=pltpu.VMEM)
    return pl.pallas_call(
        body,
        out_shape=outs,
        in_specs=[pl.BlockSpec(memory_space=pltpu.SMEM)] + [vmem] * (n_in - 1),
        out_specs=[vmem] * len(outs),
        scratch_shapes=scratch,
        compiler_params=pltpu.CompilerParams(vmem_limit_bytes=VMEM_LIMIT),
        cost_estimate=pl.CostEstimate(
            flops=flops, bytes_accessed=8 * 2**20, transcendentals=2**18
        ),
    )


def on_device(volume, kernel, bias, cotangent):
    chan, space = lax.axis_index("chan"), lax.axis_index("space")
    here_y, half, core = chan // 2, chan % 2, space % 2
    at = jnp.stack([here_y, half, core]).astype(jnp.int32)
    swap = functools.partial(
        lax.ppermute, axis_name="chan", perm=[(i, i ^ 1) for i in range(8)]
    )

    def turn(value, step):
        return lax.ppermute(value, "chan", [(i, (i + 2 * step) % 8) for i in range(8)])

    swap_core = functools.partial(
        lax.ppermute, axis_name="space", perm=[(i, i ^ 1) for i in range(16)]
    )

    def up(value):
        return lax.ppermute(value, "space", [(i, i + 1) for i in range(15)])

    def down(value):
        return lax.ppermute(value, "space", [(i + 1, i) for i in range(15)])

    below, above = up(volume[3:]), down(volume[:1])
    rimmed = jnp.concatenate([below, volume, above], axis=0)
    mine = lax.dynamic_slice_in_dim(rimmed, 7 * half, 9, axis=1)
    theirs = lax.dynamic_slice_in_dim(rimmed, 7 * (1 - half), 9, axis=1)
    got = swap(theirs)
    own = jnp.where(
        half == 0,
        jnp.concatenate([mine, got], axis=2),
        jnp.concatenate([got, mine], axis=2),
    )
    left, right = turn(own, 1), turn(own, -1)
    far_lo, far_hi = turn(left[:3], 1), turn(right[3:], -1)

    kernel_all = jnp.concatenate([kernel, swap(kernel)], axis=1)
    bias_all = jnp.concatenate([bias, swap(bias)])
    bias_wide = jnp.broadcast_to(bias_all[:, None], (64, 128))
    turned = kernel_all.reshape(27 * 64, 256).T
    cot_own = lax.dynamic_slice_in_dim(cotangent, 8 * half, 8, axis=1)
    cot_other = swap(lax.dynamic_slice_in_dim(cotangent, 8 * (1 - half), 8, axis=1))

    shape = jax.ShapeDtypeStruct
    flops = 36 * 10**8
    out_own, out_other, grad, field = call(
        forward_body, 10,
        [
            shape((4, 8, 32, 128), BF16),
            shape((4, 8, 32, 128), BF16),
            shape((4, 8, 64, 128), BF16),
            shape((6, 10, 256, 128), BF16),
        ],
        [], flops,
    )(at, own, left, right, far_lo, far_hi, kernel_all.reshape(9, 192, 256), bias_wide,
      cot_own, cot_other)

    def rows_of(first, second):
        return jnp.where(
            half == 0,
            jnp.concatenate([first, second], axis=1),
            jnp.concatenate([second, first], axis=1),
        )

    output = rows_of(out_own, swap(out_other))

    rim = lax.dynamic_index_in_dim(grad, 7 * (1 - half), axis=1, keepdims=False)
    edge = swap(jnp.concatenate([rim[:, 32:], rim[:, :32]], axis=1))
    low = up(jnp.concatenate([grad[3], edge[3:]], axis=0))
    high = down(jnp.concatenate([grad[0], edge[:1]], axis=0))

    (sums,) = call(
        weight_body, 3, [shape((2, 2, 27, 16, 256), F32)],
        [pltpu.VMEM((4, 8, 192, 128), BF16)], flops,
    )(at, field, grad)
    chip = sums[0] + swap_core(sums[1])
    pair = chip[0] + swap(chip[1])
    groups = [[2 * k + c for k in range(8)] for c in range(2)]
    pieces = lax.all_to_all(
        pair.reshape(8, 54, 256), "space", 0, 0, tiled=True, axis_index_groups=groups
    )
    whole = jnp.sum(pieces, axis=0) / math.sqrt(64 * 16 * 128)
    spread_out = lax.all_to_all(
        jnp.broadcast_to(whole[None], (8, 54, 256)), "space", 0, 0, tiled=True,
        axis_index_groups=groups,
    ).reshape(27, 16, 256)
    other = swap_core(spread_out)
    weight_grad = jnp.where(
        core == 0,
        jnp.concatenate([spread_out, other], axis=1),
        jnp.concatenate([other, spread_out], axis=1),
    )

    mine_f, parts = call(
        input_body, 6,
        [shape((4, 8, 64, 128), F32), shape((4, 4, 8, 64, 128), BF16)],
        [pltpu.VMEM((6, 10, 192, 128), BF16), pltpu.VMEM((256, 256), F32)], flops,
    )(at, grad, edge, low, high, turned)
    terms = [turn(parts[1], 1), turn(parts[3], -1), turn(parts[2], 2)]
    back = (mine_f + sum(term.astype(F32) for term in terms)).astype(BF16)
    kept = lax.dynamic_slice_in_dim(back, 32 * half, 32, axis=2)
    sent = lax.dynamic_slice_in_dim(back, 32 * (1 - half), 32, axis=2)
    input_grad = rows_of(kept, swap(sent))
    return output, input_grad, weight_grad


def solution(mesh):
    return jax.shard_map(
        on_device,
        mesh=mesh,
        in_specs=(
            P("space", None, "chan", None),
            P(None, "chan", None),
            P("chan"),
            P("space", None, "chan", None),
        ),
        out_specs=(
            P("space", None, "chan", None),
            P("space", None, "chan", None),
            P(None, "chan", None),
        ),
        check_vma=False,
    )
```

```python
import functools
import math

import jax
import jax.numpy as jnp
from jax import lax
from jax.experimental import pallas as pl
from jax.experimental.pallas import tpu as pltpu
from jax.sharding import Mesh
from jax.sharding import PartitionSpec as P

BF16 = jnp.bfloat16
F32 = jnp.float32
VMEM_LIMIT = 20 * 1024 * 1024
CHAN = ("y", "xh")
SPACE = ("z", "xl", "core")


def moved(value, step):
    if step == 0:
        return value
    size = value.shape[-1]
    lane = lax.broadcasted_iota(jnp.int32, value.shape, value.ndim - 1)
    rolled = pltpu.roll(value, step % size, value.ndim - 1)
    edge = 0 if step == 1 else size - 1
    return jnp.where(lane == edge, 0.0, rolled)


def pair_of(ref, plane, row):
    return jnp.concatenate([ref[plane, row], ref[plane, row + 1]], axis=1)


def starts_of(here_y):
    return [pl.multiple_of(lax.rem(here_y + shift, 4) * 64, 64) for shift in range(4)]


def forward_rows(row, places, kernel, bias, cot_own, cot_other, out_own, out_other, grad,
                 plane_cot, plane_out):
    outs = kernel.shape[1] // 3
    total = jnp.zeros((3 * outs, 256), F32)
    for a, (ref, plane) in enumerate(places):
        for b in range(3):
            total = total + jnp.dot(
                kernel[3 * a + b], pair_of(ref, plane, row + b), preferred_element_type=F32
            )
    for r in range(2):
        part = total[:, 128 * r : 128 * r + 128]
        pre = (
            moved(part[:outs], 1) + part[outs : 2 * outs] + moved(part[2 * outs :], -1)
            + bias[...]
        )
        sig = 1.0 / (1.0 + jnp.exp(-pre))
        out = (pre * sig).astype(BF16)
        out_own[plane_out, row + r] = out[: outs // 2]
        out_other[plane_out, row + r] = out[outs // 2 :]
        cot = jnp.concatenate(
            [cot_own[plane_cot, row + r], cot_other[plane_cot, row + r]], axis=0
        ).astype(F32)
        grad[plane_out, row + r] = (cot * sig * (1.0 + pre * (1.0 - sig))).astype(BF16)


def inner_body(at, own, left, right, far_lo, far_hi, kernel, bias, cot_own, cot_other,
               out_own, out_other, grad, field):
    half, starts = at[1], starts_of(at[0])
    rows = own.shape[1]

    def put(plane, row, shift, value):
        field[plane, row + 1 - half, pl.ds(starts[shift], 64), :] = value

    def fill(plane, carry):
        for row in range(rows):
            for shift, ref in ((0, own), (3, left), (1, right)):
                put(plane, row, shift, ref[plane, row])
        field[plane, 9 * half] = jnp.zeros(field.shape[2:], BF16)
        return carry

    lax.fori_loop(0, 4, fill, 0)

    def fill_far(plane, carry):
        for row in range(rows):
            put(plane, row, 2, far_lo[plane, row])
            put(plane + 2, row, 2, far_hi[plane, row])
        return carry

    lax.fori_loop(0, 2, fill_far, 0)

    def step(index, carry):
        plane, row = index // 4, 2 * lax.rem(index, 4)
        forward_rows(
            row, [(field, plane), (field, plane + 1), (field, plane + 2)], kernel, bias,
            cot_own, cot_other, out_own, out_other, grad, plane + 1, plane,
        )
        return carry

    lax.fori_loop(0, 8, step, 0)


def outer_body(at, field, low, low_far, high, high_far, kernel, bias, cot_own, cot_other,
               in_own, in_other, in_grad, after, out_own, out_other, grad, first, last, rim):
    half, starts = at[1], starts_of(at[0])
    rows = low_far.shape[0]
    for side, near, far in ((0, low, low_far), (1, high, high_far)):
        for row in range(rows):
            for k, shift in enumerate((0, 3, 1)):
                rim[side, row + 1 - half, pl.ds(starts[shift], 64), :] = near[k, row]
            rim[side, row + 1 - half, pl.ds(starts[2], 64), :] = far[row]
        rim[side, 9 * half] = jnp.zeros(rim.shape[2:], BF16)
    for plane in range(2):
        out_own[plane + 1] = in_own[plane]
        out_other[plane + 1] = in_other[plane]
        grad[plane + 1] = in_grad[plane]

    def step(index, carry):
        row = 2 * index
        forward_rows(
            row, [(rim, 0), (field, 0), (field, 1)], kernel, bias,
            cot_own, cot_other, out_own, out_other, grad, 0, 0,
        )
        forward_rows(
            row, [(field, 2), (field, 3), (rim, 1)], kernel, bias,
            cot_own, cot_other, out_own, out_other, grad, 3, 3,
        )
        for r in range(2):
            first[row + r] = grad[0, row + r]
            last[row + r] = grad[3, row + r]
        return carry

    lax.fori_loop(0, 4, step, 0)


def spread(line):
    wide = line.astype(F32)
    return [moved(wide, c - 1).astype(BF16) for c in range(3)]


def weight_body(at, field, rim, grad, keep, give, stacked):
    half, core = at[1], at[2]
    planes, rows, outs = grad.shape[0], grad.shape[1], grad.shape[2]

    def fill(plane, carry):
        for row in range(rows):
            for c, line in enumerate(spread(grad[plane, row])):
                stacked[plane, row, outs * c : outs * (c + 1), :] = line
        return carry

    lax.fori_loop(0, planes, fill, 0)
    for side in range(2):
        for ref in (keep, give):
            ref[side, 432:448, :] = jnp.zeros((16, 256), F32)

    def cells_of(plane, b):
        if plane == 0:
            ref, plane = rim, 0
        elif plane == 5:
            ref, plane = rim, 1
        else:
            ref, plane = field, plane - 1
        return jnp.concatenate([ref[plane, row + b] for row in range(rows)], axis=1)

    for a in range(3):

        def step(b, carry):
            total = jnp.zeros((3 * outs, 256), F32)
            for plane in range(planes):
                grads = jnp.concatenate([stacked[plane, row] for row in range(rows)], axis=1)
                total = total + lax.dot_general(
                    grads, cells_of(plane + a, b), (((1,), (1,)), ((), ())),
                    preferred_element_type=F32,
                )
            for c in range(3):
                line = pl.multiple_of(16 * (9 * a + 3 * b + c), 16)
                for side in range(2):
                    low = outs * c + 32 * side
                    parts = total[low : low + 16], total[low + 16 : low + 32]
                    kept = jnp.where(core == 0, parts[0], parts[1])
                    given = jnp.where(core == 0, parts[1], parts[0])
                    keep[side ^ half, pl.ds(line, 16), :] = kept
                    give[side ^ half, pl.ds(line, 16), :] = given
            return carry

        lax.fori_loop(0, 3, step, 0)


def input_body(chunk, at, grad, rim, turned, turned_edge, after, own, near, far, back,
               stacked, held):
    half, starts = at[1], starts_of(at[0])
    rows, outs = grad.shape[1], grad.shape[2]

    def put(plane, row, line):
        for c, value in enumerate(spread(line)):
            stacked[plane, row, outs * c : outs * (c + 1), :] = value

    first, outer = (1, 0) if chunk == 0 else (0, 3)

    def fill(k, carry):
        for row in range(rows):
            put(k + first, row + 1, grad[k + chunk, row])
        return carry

    lax.fori_loop(0, 3, fill, 0)
    for row in range(rows):
        put(outer, row + 1, rim[row])
    for plane in range(4):
        for row in (0, 9):
            stacked[plane, row] = jnp.zeros(stacked.shape[2:], BF16)

    def store(places):
        for start, ref in zip(starts, (own, near, far, back)):
            block = held[pl.ds(start, 64), :]
            for r, (plane, row) in enumerate(places):
                ref[plane, row] = block[:, 128 * r : 128 * r + 128].astype(ref.dtype)

    def step(index, carry):
        plane, row = index // 4, 2 * lax.rem(index, 4)
        terms = jnp.concatenate(
            [
                pair_of(stacked, plane + 2 - a, row + 2 - b)
                for a in range(3)
                for b in range(3)
            ],
            axis=0,
        )
        held[...] = jnp.dot(turned[...], terms, preferred_element_type=F32)
        store([(plane, row), (plane, row + 1)])
        return carry

    lax.fori_loop(0, 8, step, 0)
    nearest = 8 - 7 * half
    terms = jnp.concatenate(
        [
            jnp.concatenate([stacked[2 - a, nearest], stacked[3 - a, nearest]], axis=1)
            for a in range(3)
        ],
        axis=0,
    )
    held[...] = jnp.dot(turned_edge[...], terms, preferred_element_type=F32)
    store([(0, rows), (1, rows)])


def total_body(at, own, near, far, back, kept, sent):
    half = at[1]
    mine = pl.multiple_of(32 * half, 32)
    others = pl.multiple_of(32 * (1 - half), 32)

    def sums(plane, row, start):
        value = own[plane, row, pl.ds(start, 32), :]
        for ref in (near, far, back):
            value = value + ref[plane, row, pl.ds(start, 32), :].astype(F32)
        return value

    for plane in range(2):
        for row in range(9):
            kept[plane, row] = sums(plane, row, mine)
            sent[plane, row] = sums(plane, row, others).astype(BF16)


def join_body(at, kept_0, kept_1, got_0, got_1, joined):
    half = at[1]
    for k, (kept, got) in enumerate(((kept_0, got_0), (kept_1, got_1))):
        for plane in range(2):
            for row in range(8):
                joined[2 * k + plane, 8 * half + row] = kept[plane, row].astype(BF16)
                joined[2 * k + plane, 8 - 8 * half + row] = got[plane, row]
            beside = 7 * (1 - half)
            joined[2 * k + plane, 8 * half + beside] = (
                kept[plane, beside] + got[plane, 8].astype(F32)
            ).astype(BF16)
            beyond = 7 * half
            joined[2 * k + plane, 8 - 8 * half + beyond] = (
                kept[plane, 8] + got[plane, beyond].astype(F32)
            ).astype(BF16)


def call(body, n_in, outs, scratch, flops, after=0):
    vmem = pl.BlockSpec(memory_space=pltpu.VMEM)
    anywhere = pl.BlockSpec(memory_space=pl.ANY)
    return pl.pallas_call(
        body,
        out_shape=[jax.ShapeDtypeStruct(*out) for out in outs],
        in_specs=[pl.BlockSpec(memory_space=pltpu.SMEM)]
        + [vmem] * (n_in - 1)
        + [anywhere] * after,
        out_specs=[vmem] * len(outs),
        scratch_shapes=scratch,
        compiler_params=pltpu.CompilerParams(vmem_limit_bytes=VMEM_LIMIT),
        cost_estimate=pl.CostEstimate(
            flops=flops, bytes_accessed=8 * 2**20, transcendentals=2**18
        ),
    )


def on_device(volume, kernel, bias, cotangent):
    here_y, half, core = lax.axis_index("y"), lax.axis_index("xh"), lax.axis_index("core")
    at = jnp.stack([here_y, half, core]).astype(jnp.int32)

    def swap(value):
        return lax.ppermute(value, "xh", [(0, 1), (1, 0)])

    def swap_core(value):
        return lax.ppermute(value, "core", [(0, 1), (1, 0)])

    def turn(value, step):
        return lax.ppermute(value, "y", [(i, (i + step) % 4) for i in range(4)])

    def up(value):
        return lax.ppermute(value, SPACE, [(i, i + 1) for i in range(15)])

    def down(value):
        return lax.ppermute(value, SPACE, [(i + 1, i) for i in range(15)])

    mine = lax.dynamic_slice_in_dim(volume, 7 * half, 9, axis=1)
    got = swap(lax.dynamic_slice_in_dim(volume, 7 * (1 - half), 9, axis=1))
    own = jnp.where(
        half == 0,
        jnp.concatenate([mine, got], axis=2),
        jnp.concatenate([got, mine], axis=2),
    )
    left, right = turn(own, 1), turn(own, -1)
    far_lo, far_hi = turn(left[:2], 1), turn(right[2:], -1)
    low = up(jnp.concatenate([own[3:], left[3:], right[3:]], axis=0))
    high = down(jnp.concatenate([own[:1], left[:1], right[:1]], axis=0))
    low_far, high_far = up(far_hi[1]), down(far_lo[0])

    kernel_all = jnp.concatenate([kernel, swap(kernel)], axis=1)
    taps = kernel_all.reshape(9, 192, 256)
    bias_all = jnp.concatenate([bias, swap(bias)])
    bias_wide = jnp.broadcast_to(bias_all[:, None], (64, 128))
    turned = kernel_all.reshape(27 * 64, 256).T
    by_b = taps.reshape(3, 3, 192, 256)
    turned_edge = jnp.where(half == 0, by_b[:, 2], by_b[:, 0]).reshape(576, 256).T
    cot_own = lax.dynamic_slice_in_dim(cotangent, 8 * half, 8, axis=1)
    cot_other = swap(lax.dynamic_slice_in_dim(cotangent, 8 * (1 - half), 8, axis=1))

    flops = 36 * 10**8
    out_own, out_other, grad, field = call(
        inner_body, 10,
        [
            ((2, 8, 32, 128), BF16), ((2, 8, 32, 128), BF16), ((2, 8, 64, 128), BF16),
            ((4, 10, 256, 128), BF16),
        ],
        [], flops // 2,
    )(at, own, left, right, far_lo, far_hi, taps, bias_wide, cot_own, cot_other)
    out_own, out_other, grad, first, last, rim = call(
        outer_body, 13,
        [
            ((4, 8, 32, 128), BF16), ((4, 8, 32, 128), BF16), ((4, 8, 64, 128), BF16),
            ((8, 64, 128), BF16), ((8, 64, 128), BF16), ((2, 10, 256, 128), BF16),
        ],
        [], flops // 2, 1,
    )(at, field, low, low_far, high, high_far, taps, bias_wide, cot_own, cot_other,
      out_own, out_other, grad, turned)

    got_out = swap(out_other)
    output = jnp.where(
        half == 0,
        jnp.concatenate([out_own, got_out], axis=1),
        jnp.concatenate([got_out, out_own], axis=1),
    )
    grad_low, grad_high = up(last), down(first)

    keep, give = call(
        weight_body, 4, [((2, 448, 256), F32)] * 2,
        [pltpu.VMEM((4, 8, 192, 128), BF16)], flops,
    )(at, field, rim, grad)
    chip = (keep + swap_core(give)).reshape(16, 56, 256)
    pieces = lax.all_to_all(chip, ("xh", "z", "xl"), 0, 0, tiled=True)
    whole = jnp.sum(pieces, axis=0) / math.sqrt(64 * 16 * 128)
    everyone = lax.all_to_all(
        jnp.broadcast_to(whole[None], (8, 56, 256)), ("z", "xl"), 0, 0, tiled=True
    ).reshape(448, 256)
    other = swap_core(everyone)
    everyone, other = (v[:432].reshape(27, 16, 256) for v in (everyone, other))
    weight_grad = jnp.where(
        core == 0,
        jnp.concatenate([everyone, other], axis=1),
        jnp.concatenate([other, everyone], axis=1),
    )

    def input_chunk(chunk, rim, after):
        own, near, far, back = call(
            functools.partial(input_body, chunk), 5,
            [((2, 9, 64, 128), F32)] + [((2, 9, 64, 128), BF16)] * 3,
            [pltpu.VMEM((4, 10, 192, 128), BF16), pltpu.VMEM((256, 256), F32)],
            flops // 2, 1,
        )(at, grad, rim, turned, turned_edge, after)
        near, back, far = turn(near, 1), turn(back, -1), turn(far, 2)
        kept, sent = call(
            total_body, 5, [((2, 9, 32, 128), F32), ((2, 9, 32, 128), BF16)], [], 10**6
        )(at, own, near, far, back)
        return kept, swap(sent)

    kept_0, got_0 = input_chunk(0, grad_low, bias_wide)
    kept_1, got_1 = input_chunk(1, grad_high, output)
    (input_grad,) = call(join_body, 5, [((4, 16, 32, 128), BF16)], [], 10**6)(
        at, kept_0, kept_1, got_0, got_1
    )
    return output, input_grad, weight_grad


def solution(mesh):
    split = Mesh(mesh.devices.reshape(4, 2, 4, 2, 2), CHAN + SPACE)
    return jax.shard_map(
        on_device,
        mesh=split,
        in_specs=(
            P(SPACE, None, CHAN, None),
            P(None, CHAN, None),
            P(CHAN),
            P(SPACE, None, CHAN, None),
        ),
        out_specs=(
            P(SPACE, None, CHAN, None),
            P(SPACE, None, CHAN, None),
            P(None, CHAN, None),
        ),
        check_vma=False,
    )
```

```python
import functools
import math

import jax
import jax.numpy as jnp
from jax import lax
from jax.experimental import pallas as pl
from jax.experimental.pallas import tpu as pltpu
from jax.sharding import Mesh
from jax.sharding import PartitionSpec as P

BF16 = jnp.bfloat16
F32 = jnp.float32
VMEM_LIMIT = 20 * 1024 * 1024
CHAN = ("y", "xh")
SPACE = ("z", "xl", "core")


def moved(value, step):
    if step == 0:
        return value
    size = value.shape[-1]
    lane = lax.broadcasted_iota(jnp.int32, value.shape, value.ndim - 1)
    rolled = pltpu.roll(value, step % size, value.ndim - 1)
    edge = 0 if step == 1 else size - 1
    return jnp.where(lane == edge, 0.0, rolled)


def pair_of(ref, plane, row):
    return jnp.concatenate([ref[plane, row], ref[plane, row + 1]], axis=1)


def starts_of(here_y):
    return [pl.multiple_of(lax.rem(here_y + shift, 4) * 64, 64) for shift in range(4)]


def forward_rows(row, places, kernel, bias, cot_own, cot_other, out_own, out_other, grad,
                 plane_cot, plane_out):
    outs = kernel.shape[1] // 3
    total = jnp.zeros((3 * outs, 256), F32)
    for a, (ref, plane) in enumerate(places):
        for b in range(3):
            total = total + jnp.dot(
                kernel[3 * a + b], pair_of(ref, plane, row + b), preferred_element_type=F32
            )
    for r in range(2):
        part = total[:, 128 * r : 128 * r + 128]
        pre = (
            moved(part[:outs], 1) + part[outs : 2 * outs] + moved(part[2 * outs :], -1)
            + bias[...]
        )
        sig = 1.0 / (1.0 + jnp.exp(-pre))
        out = (pre * sig).astype(BF16)
        out_own[plane_out, row + r] = out[: outs // 2]
        out_other[plane_out, row + r] = out[outs // 2 :]
        cot = jnp.concatenate(
            [cot_own[plane_cot, row + r], cot_other[plane_cot, row + r]], axis=0
        ).astype(F32)
        grad[plane_out, row + r] = (cot * sig * (1.0 + pre * (1.0 - sig))).astype(BF16)


def ready_body(at, kernel, bias, cotangent, after, kernel_out, cot_own, cot_sent):
    half = at[1]
    kernel_out[:27] = kernel[...]
    rest = bias[...]
    for k in range(3):
        part = rest.astype(BF16)
        kernel_out[27 + k // 2, :, 128 * (k % 2) : 128 * (k % 2) + 128] = part
        rest = rest - part.astype(F32)
    kernel_out[28, :, 128:] = jnp.zeros((32, 128), BF16)
    for plane in range(4):
        for row in range(8):
            cot_own[plane, row] = cotangent[plane, 8 * half + row]
            cot_sent[plane, row] = cotangent[plane, 8 - 8 * half + row]


def rims_body(at, own_lo, own_hi, left_lo, left_hi, right_lo, right_hi, far_lo, far_hi,
              kernel, cot, up_rim, down_rim):
    for k, (lower, upper) in enumerate(
        ((own_lo, own_hi), (right_lo, right_hi), (far_lo, far_hi), (left_lo, left_hi))
    ):
        up_rim[k] = upper[1]
        down_rim[k] = lower[0]


def inner_body(at, own_lo, own_hi, left_lo, left_hi, right_lo, right_hi, far_lo, far_hi,
               kernel_own, kernel_other, cot_own, cot_other, out_own, out_other, grad,
               field, kernel, bias):
    half, starts = at[1], starts_of(at[0])
    rows = own_lo.shape[1]

    def fill_kernel(ab, carry):
        for c in range(3):
            kernel[ab, 64 * c : 64 * c + 32] = kernel_own[3 * ab + c]
            kernel[ab, 64 * c + 32 : 64 * c + 64] = kernel_other[3 * ab + c]
        return carry

    lax.fori_loop(0, 9, fill_kernel, 0)
    for k, ref in enumerate((kernel_own, kernel_other)):
        bias[32 * k : 32 * k + 32] = (
            ref[27, :, :128].astype(F32) + ref[27, :, 128:].astype(F32)
        ) + ref[28, :, :128].astype(F32)
    sources = (own_lo, own_hi), (right_lo, right_hi), (far_lo, far_hi), (left_lo, left_hi)

    def fill(k, carry):
        for upper in range(2):
            plane = k + 2 * upper
            for row in range(rows):
                for start, pair in zip(starts, sources):
                    field[plane, row + 1 - half, pl.ds(start, 64), :] = pair[upper][k, row]
            field[plane, 9 * half] = jnp.zeros(field.shape[2:], BF16)
        return carry

    lax.fori_loop(0, 2, fill, 0)

    def step(index, carry):
        plane, row = index // 4, 2 * lax.rem(index, 4)
        forward_rows(
            row, [(field, plane), (field, plane + 1), (field, plane + 2)], kernel, bias,
            cot_own, cot_other, out_own, out_other, grad, plane + 1, plane,
        )
        return carry

    lax.fori_loop(0, 8, step, 0)


def outer_body(at, field, low, high, kernel, bias, cot_own, cot_other,
               in_own, in_other, in_grad, after, out_own, out_other, grad, first, last, rim):
    half, starts = at[1], starts_of(at[0])
    for side, ref in ((0, low), (1, high)):
        for row in range(ref.shape[1]):
            for k, start in enumerate(starts):
                rim[side, row + 1 - half, pl.ds(start, 64), :] = ref[k, row]
        rim[side, 9 * half] = jnp.zeros(rim.shape[2:], BF16)
    for plane in range(2):
        out_own[plane + 1] = in_own[plane]
        out_other[plane + 1] = in_other[plane]
        grad[plane + 1] = in_grad[plane]

    def step(index, carry):
        row = 2 * index
        forward_rows(
            row, [(rim, 0), (field, 0), (field, 1)], kernel, bias,
            cot_own, cot_other, out_own, out_other, grad, 0, 0,
        )
        forward_rows(
            row, [(field, 2), (field, 3), (rim, 1)], kernel, bias,
            cot_own, cot_other, out_own, out_other, grad, 3, 3,
        )
        for r in range(2):
            first[row + r] = grad[0, row + r]
            last[row + r] = grad[3, row + r]
        return carry

    lax.fori_loop(0, 4, step, 0)


def spread(line):
    wide = line.astype(F32)
    return [moved(wide, c - 1).astype(BF16) for c in range(3)]


def weight_sums(at, planes, grad_of, cells_of, store, stacked):
    rows, outs = stacked.shape[1], stacked.shape[2] // 3
    for k in range(planes):
        for row in range(rows):
            for c, line in enumerate(spread(grad_of(k, row))):
                stacked[k, row, outs * c : outs * (c + 1), :] = line
    for a in range(3):

        def step(b, carry):
            total = jnp.zeros((3 * outs, 256), F32)
            for k in range(planes):
                grads = jnp.concatenate([stacked[k, row] for row in range(rows)], axis=1)
                ref, plane = cells_of(k, a)
                cells = jnp.concatenate([ref[plane, row + b] for row in range(rows)], axis=1)
                total = total + lax.dot_general(
                    grads, cells, (((1,), (1,)), ((), ())), preferred_element_type=F32
                )
            for c in range(3):
                line = pl.multiple_of(16 * (9 * a + 3 * b + c), 16)
                for side in range(2):
                    low = outs * c + 32 * side
                    parts = total[low : low + 16], total[low + 16 : low + 32]
                    kept = jnp.where(at[2] == 0, parts[0], parts[1])
                    given = jnp.where(at[2] == 0, parts[1], parts[0])
                    store(side ^ at[1], pl.ds(line, 16), kept, given)
            return carry

        lax.fori_loop(0, 3, step, 0)


def inner_weight_body(at, field, grad, kernel, keep, give, turned, turned_edge, stacked):
    width = kernel.shape[1]
    wide = [kernel[ab] for ab in range(9)]
    for k in range(0, 8, 2):
        turned[:, width * k : width * (k + 2)] = jnp.concatenate(wide[k : k + 2], axis=0).T
    turned[:, 8 * width :] = wide[8].T
    beside = [
        jnp.where(at[1] == 0, kernel[3 * a + 2], kernel[3 * a]) for a in range(3)
    ]
    turned_edge[...] = jnp.concatenate(beside, axis=0).T

    def store(side, lines, kept, given):
        keep[side, lines, :] = kept
        give[side, lines, :] = given

    weight_sums(
        at, 2, lambda k, row: grad[k, row], lambda k, a: (field, k + a), store, stacked
    )


def outer_weight_body(at, field, rim, grad, in_keep, in_give, after, keep, give, stacked):
    for side in range(2):
        for ref in (keep, give):
            ref[side, 432:448, :] = jnp.zeros((16, 256), F32)

    def store(side, lines, kept, given):
        keep[side, lines, :] = kept + in_keep[side, lines, :]
        give[side, lines, :] = given + in_give[side, lines, :]

    places = [[(rim, 0), (field, 0), (field, 1)], [(field, 2), (field, 3), (rim, 1)]]
    weight_sums(
        at, 2, lambda k, row: grad[3 * k, row], lambda k, a: places[k][a], store, stacked
    )


def input_terms(at, lines, planes, turned, turned_edge, outs, stacked, held):
    half, starts = at[1], starts_of(at[0])
    rows, width = 8, stacked.shape[2] // 3
    for plane, line_of in enumerate(lines):
        for row in range(rows):
            for c, value in enumerate(spread(line_of(row))):
                stacked[plane, row + 1, width * c : width * (c + 1), :] = value
        for row in (0, 9):
            stacked[plane, row] = jnp.zeros(stacked.shape[2:], BF16)

    def store(places):
        for start, ref in zip(starts, outs):
            block = held[pl.ds(start, 64), :]
            for r, (plane, row) in enumerate(places):
                ref[plane, row] = block[:, 128 * r : 128 * r + 128].astype(ref.dtype)

    def step(index, carry):
        row = 2 * index
        for first, plane in planes:
            terms = jnp.concatenate(
                [
                    pair_of(stacked, first + 2 - a, row + 2 - b)
                    for a in range(3)
                    for b in range(3)
                ],
                axis=0,
            )
            held[...] = jnp.dot(turned[...], terms, preferred_element_type=F32)
            store([(plane, row), (plane, row + 1)])
        return carry

    lax.fori_loop(0, rows // 2, step, 0)
    nearest = 8 - 7 * half
    terms = jnp.concatenate(
        [
            jnp.concatenate([stacked[first + 2 - a, nearest] for first, _ in planes], axis=1)
            for a in range(3)
        ],
        axis=0,
    )
    held[...] = jnp.dot(turned_edge[...], terms, preferred_element_type=F32)
    store([(plane, rows) for _, plane in planes])


def inner_input_body(at, grad, turned, turned_edge, own, near, far, back, stacked, held):
    lines = [lambda row, k=k: grad[k, row] for k in range(4)]
    input_terms(
        at, lines, [(0, 0), (1, 1)], turned, turned_edge, (own, near, far, back), stacked, held
    )


def outer_input_body(at, grad, low, high, turned, turned_edge, *refs):
    given, outs, (stacked, held) = refs[:4], refs[4:8], refs[8:]
    for source, ref in zip(given, outs):
        for plane in range(2):
            ref[plane + 1] = source[plane]
    lines = [lambda row, k=k: grad[k, row] for k in range(4)]
    lines = [lambda row: low[row]] + lines + [lambda row: high[row]]
    input_terms(at, lines, [(0, 0), (3, 3)], turned, turned_edge, outs, stacked, held)


def total_body(at, own, near, far, back, kept, sent):
    half = at[1]
    mine = pl.multiple_of(32 * half, 32)
    others = pl.multiple_of(32 * (1 - half), 32)

    def sums(plane, row, start):
        value = own[plane, row, pl.ds(start, 32), :]
        for ref in (near, far, back):
            value = value + ref[plane, row, pl.ds(start, 32), :].astype(F32)
        return value

    for plane in range(4):
        for row in range(9):
            kept[plane, row] = sums(plane, row, mine)
            sent[plane, row] = sums(plane, row, others).astype(BF16)


def join_body(at, kept, got, joined):
    half = at[1]
    for plane in range(4):
        for row in range(8):
            joined[plane, 8 * half + row] = kept[plane, row].astype(BF16)
            joined[plane, 8 - 8 * half + row] = got[plane, row]
        beside = 7 * (1 - half)
        joined[plane, 8 * half + beside] = (
            kept[plane, beside] + got[plane, 8].astype(F32)
        ).astype(BF16)
        beyond = 7 * half
        joined[plane, 8 - 8 * half + beyond] = (
            kept[plane, 8] + got[plane, beyond].astype(F32)
        ).astype(BF16)


def add_body(at, keep, got, chip):
    chip[...] = keep[...] + got[...]


def mean_body(at, pieces, copies):
    total = pieces[0]
    for k in range(1, pieces.shape[0]):
        total = total + pieces[k]
    total = total * (1.0 / math.sqrt(64 * 16 * 128))
    for k in range(copies.shape[0]):
        copies[k] = total


def weave_body(at, mine, other, joined):
    core = at[2]
    for tap in range(27):
        first, second = (ref[16 * tap : 16 * tap + 16] for ref in (mine, other))
        joined[tap, :16] = jnp.where(core == 0, first, second)
        joined[tap, 16:] = jnp.where(core == 0, second, first)


def call(body, n_in, outs, scratch, flops, after=0):
    vmem = pl.BlockSpec(memory_space=pltpu.VMEM)
    anywhere = pl.BlockSpec(memory_space=pl.ANY)
    return pl.pallas_call(
        body,
        out_shape=[jax.ShapeDtypeStruct(*out) for out in outs],
        in_specs=[pl.BlockSpec(memory_space=pltpu.SMEM)]
        + [vmem] * (n_in - 1)
        + [anywhere] * after,
        out_specs=[vmem] * len(outs),
        scratch_shapes=scratch,
        compiler_params=pltpu.CompilerParams(vmem_limit_bytes=VMEM_LIMIT),
        cost_estimate=pl.CostEstimate(
            flops=flops, bytes_accessed=8 * 2**20, transcendentals=2**18
        ),
    )


def on_device(volume, kernel, bias, cotangent):
    here_y, half, core = lax.axis_index("y"), lax.axis_index("xh"), lax.axis_index("core")
    at = jnp.stack([here_y, half, core]).astype(jnp.int32)

    def swap(value):
        return lax.ppermute(value, "xh", [(0, 1), (1, 0)])

    def swap_core(value):
        return lax.ppermute(value, "core", [(0, 1), (1, 0)])

    def turn(value, step):
        return lax.ppermute(value, "y", [(i, (i + step) % 4) for i in range(4)])

    def up(value):
        return lax.ppermute(value, SPACE, [(i, i + 1) for i in range(15)])

    def down(value):
        return lax.ppermute(value, SPACE, [(i + 1, i) for i in range(15)])

    mine = lax.dynamic_slice_in_dim(volume, 7 * half, 9, axis=1)
    got = swap(lax.dynamic_slice_in_dim(volume, 7 * (1 - half), 9, axis=1))
    own_lo, own_hi = (
        jnp.where(
            half == 0,
            jnp.concatenate([mine[k : k + 2], got[k : k + 2]], axis=2),
            jnp.concatenate([got[k : k + 2], mine[k : k + 2]], axis=2),
        )
        for k in (0, 2)
    )
    left_lo, right_hi = turn(own_lo, 1), turn(own_hi, -1)
    left_hi, right_lo = turn(own_hi, 1), turn(own_lo, -1)
    far_lo, far_hi = turn(left_lo, 1), turn(right_hi, -1)
    kernel_sent, cot_own, cot_sent = call(
        ready_body, 4,
        [((29, 32, 256), BF16), ((4, 8, 32, 128), BF16), ((4, 8, 32, 128), BF16)],
        [], 10**6, 1,
    )(at, kernel, jnp.broadcast_to(bias[:, None], (32, 128)), cotangent, own_lo)
    kernel_other, cot_other = swap(kernel_sent), swap(cot_sent)
    up_rim, down_rim = call(rims_body, 9, [((4, 9, 64, 128), BF16)] * 2, [], 10**6, 2)(
        at, own_lo, own_hi, left_lo, left_hi, right_lo, right_hi, far_lo, far_hi,
        kernel_other, cot_other,
    )
    low, high = up(up_rim), down(down_rim)

    flops = 36 * 10**8
    out_own, out_other, grad, field, taps, bias_wide = call(
        inner_body, 13,
        [
            ((2, 8, 32, 128), BF16), ((2, 8, 32, 128), BF16), ((2, 8, 64, 128), BF16),
            ((4, 10, 256, 128), BF16), ((9, 192, 256), BF16),
            ((64, 128), F32),
        ],
        [], flops // 2,
    )(at, own_lo, own_hi, left_lo, left_hi, right_lo, right_hi, far_lo, far_hi,
      kernel_sent, kernel_other, cot_own, cot_other)
    keep, give, turned, turned_edge = call(
        inner_weight_body, 4,
        [((2, 448, 256), F32)] * 2 + [((256, 1728), BF16), ((256, 576), BF16)],
        [pltpu.VMEM((2, 8, 192, 128), BF16)], flops // 2,
    )(at, field, grad, taps)
    out_own, out_other, grad, first, last, rim = call(
        outer_body, 11,
        [
            ((4, 8, 32, 128), BF16), ((4, 8, 32, 128), BF16), ((4, 8, 64, 128), BF16),
            ((8, 64, 128), BF16), ((8, 64, 128), BF16), ((2, 10, 256, 128), BF16),
        ],
        [], flops // 2, 1,
    )(at, field, low, high, taps, bias_wide, cot_own, cot_other,
      out_own, out_other, grad, keep)

    got_out = swap(out_other)
    output = jnp.where(
        half == 0,
        jnp.concatenate([out_own, got_out], axis=1),
        jnp.concatenate([got_out, out_own], axis=1),
    )
    grad_low, grad_high = up(last), down(first)

    def input_chunk(chunk, rim):
        return call(
            functools.partial(input_body, chunk), 5,
            [((2, 9, 64, 128), F32)] + [((2, 9, 64, 128), BF16)] * 3,
            [pltpu.VMEM((4, 10, 192, 128), BF16), pltpu.VMEM((256, 256), F32)],
            flops // 2,
        )(at, grad, rim, turned, turned_edge)

    def total_chunk(own, near, far, back):
        near, back, far = turn(near, 1), turn(back, -1), turn(far, 2)
        kept, sent = call(
            total_body, 5, [((2, 9, 32, 128), F32), ((2, 9, 32, 128), BF16)], [], 10**6
        )(at, own, near, far, back)
        return kept, sent, swap(sent)

    def input_shapes(planes):
        return [((planes, 9, 64, 128), F32)] + [((planes, 9, 64, 128), BF16)] * 3

    def input_scratch(planes):
        return [pltpu.VMEM((planes, 10, 192, 128), BF16), pltpu.VMEM((256, 256), F32)]

    parts = call(
        inner_input_body, 4, input_shapes(2), input_scratch(4), flops // 2
    )(at, grad, turned, turned_edge)
    own, near, far, back = call(
        outer_input_body, 10, input_shapes(4), input_scratch(6), flops // 2
    )(at, grad, grad_low, grad_high, turned, turned_edge, *parts)
    keep, give = call(
        outer_weight_body, 6, [((2, 448, 256), F32)] * 2,
        [pltpu.VMEM((2, 8, 192, 128), BF16)], flops // 2, 1,
    )(at, field, rim, grad, keep, give, near)
    near, back, far = turn(near, 1), turn(back, -1), turn(far, 2)
    kept, sent = call(
        total_body, 5, [((4, 9, 32, 128), F32), ((4, 9, 32, 128), BF16)], [], 10**6
    )(at, own, near, far, back)
    got = swap(sent)
    (chip,) = call(add_body, 3, [((2, 448, 256), F32)], [], 10**6)(
        at, keep, swap_core(give)
    )
    pieces = lax.all_to_all(
        chip.reshape(16, 56, 256), ("xh", "z", "xl"), 0, 0, tiled=True
    )
    (copies,) = call(mean_body, 2, [((8, 56, 256), F32)], [], 10**6)(at, pieces)
    everyone = lax.all_to_all(copies, ("z", "xl"), 0, 0, tiled=True).reshape(448, 256)
    (weight_grad,) = call(weave_body, 3, [((27, 32, 256), F32)], [], 10**6)(
        at, everyone, swap_core(everyone)
    )
    (input_grad,) = call(join_body, 3, [((4, 16, 32, 128), BF16)], [], 10**6)(at, kept, got)
    return output, input_grad, weight_grad


def solution(mesh):
    split = Mesh(mesh.devices.reshape(4, 2, 4, 2, 2), CHAN + SPACE)
    return jax.shard_map(
        on_device,
        mesh=split,
        in_specs=(
            P(SPACE, None, CHAN, None),
            P(None, CHAN, None),
            P(CHAN),
            P(SPACE, None, CHAN, None),
        ),
        out_specs=(
            P(SPACE, None, CHAN, None),
            P(SPACE, None, CHAN, None),
            P(None, CHAN, None),
        ),
        check_vma=False,
    )
```

```python
import functools
import math

import jax
import jax.numpy as jnp
from jax import lax
from jax.experimental import pallas as pl
from jax.experimental.pallas import tpu as pltpu
from jax.sharding import Mesh
from jax.sharding import PartitionSpec as P

BF16 = jnp.bfloat16
F32 = jnp.float32
VMEM_LIMIT = 20 * 1024 * 1024
CHAN = ("y", "xh")
SPACE = ("z", "xl", "core")


def moved(value, step):
    if step == 0:
        return value
    size = value.shape[-1]
    lane = lax.broadcasted_iota(jnp.int32, value.shape, value.ndim - 1)
    rolled = pltpu.roll(value, step % size, value.ndim - 1)
    edge = 0 if step == 1 else size - 1
    return jnp.where(lane == edge, 0.0, rolled)


def pair_of(ref, plane, row):
    return jnp.concatenate([ref[plane, row], ref[plane, row + 1]], axis=1)


def starts_of(here_y):
    return [pl.multiple_of(lax.rem(here_y + shift, 4) * 64, 64) for shift in range(4)]


def forward_rows(row, places, kernel, bias, cot_own, cot_other, out_own, out_other, grad,
                 plane_cot, plane_out):
    outs = kernel.shape[1] // 3
    total = jnp.zeros((3 * outs, 256), F32)
    for a, (ref, plane) in enumerate(places):
        for b in range(3):
            total = total + jnp.dot(
                kernel[3 * a + b], pair_of(ref, plane, row + b), preferred_element_type=F32
            )
    for r in range(2):
        part = total[:, 128 * r : 128 * r + 128]
        pre = (
            moved(part[:outs], 1) + part[outs : 2 * outs] + moved(part[2 * outs :], -1)
            + bias[...]
        )
        sig = 1.0 / (1.0 + jnp.exp(-pre))
        out = (pre * sig).astype(BF16)
        out_own[plane_out, row + r] = out[: outs // 2]
        out_other[plane_out, row + r] = out[outs // 2 :]
        cot = jnp.concatenate(
            [cot_own[plane_cot, row + r], cot_other[plane_cot, row + r]], axis=0
        ).astype(F32)
        grad[plane_out, row + r] = (cot * sig * (1.0 + pre * (1.0 - sig))).astype(BF16)


def ready_body(at, kernel, bias, cotangent, after, kernel_out, cot_own, cot_sent):
    half = at[1]
    kernel_out[:27] = kernel[...]
    rest = bias[...]
    for k in range(3):
        part = rest.astype(BF16)
        kernel_out[27 + k // 2, :, 128 * (k % 2) : 128 * (k % 2) + 128] = part
        rest = rest - part.astype(F32)
    kernel_out[28, :, 128:] = jnp.zeros((32, 128), BF16)
    for plane in range(4):
        for row in range(8):
            cot_own[plane, row] = cotangent[plane, 8 * half + row]
            cot_sent[plane, row] = cotangent[plane, 8 - 8 * half + row]


def rims_body(at, own_lo, own_hi, left_lo, left_hi, right_lo, right_hi, far_lo, far_hi,
              kernel, cot, up_rim, down_rim):
    for k, (lower, upper) in enumerate(
        ((own_lo, own_hi), (right_lo, right_hi), (far_lo, far_hi), (left_lo, left_hi))
    ):
        up_rim[k] = upper[1]
        down_rim[k] = lower[0]


def inner_body(at, own_lo, own_hi, left_lo, left_hi, right_lo, right_hi, far_lo, far_hi,
               kernel_own, kernel_other, cot_own, cot_other, out_own, out_other, grad,
               field, kernel, bias):
    half, starts = at[1], starts_of(at[0])
    rows = own_lo.shape[1]

    def fill_kernel(ab, carry):
        for c in range(3):
            kernel[ab, 64 * c : 64 * c + 32] = kernel_own[3 * ab + c]
            kernel[ab, 64 * c + 32 : 64 * c + 64] = kernel_other[3 * ab + c]
        return carry

    lax.fori_loop(0, 9, fill_kernel, 0)
    for k, ref in enumerate((kernel_own, kernel_other)):
        bias[32 * k : 32 * k + 32] = (
            ref[27, :, :128].astype(F32) + ref[27, :, 128:].astype(F32)
        ) + ref[28, :, :128].astype(F32)
    sources = (own_lo, own_hi), (right_lo, right_hi), (far_lo, far_hi), (left_lo, left_hi)

    def fill(k, carry):
        for upper in range(2):
            plane = k + 2 * upper
            for row in range(rows):
                for start, pair in zip(starts, sources):
                    field[plane, row + 1 - half, pl.ds(start, 64), :] = pair[upper][k, row]
            field[plane, 9 * half] = jnp.zeros(field.shape[2:], BF16)
        return carry

    lax.fori_loop(0, 2, fill, 0)

    def step(index, carry):
        plane, row = index // 4, 2 * lax.rem(index, 4)
        forward_rows(
            row, [(field, plane), (field, plane + 1), (field, plane + 2)], kernel, bias,
            cot_own, cot_other, out_own, out_other, grad, plane + 1, plane,
        )
        return carry

    lax.fori_loop(0, 8, step, 0)


def outer_body(at, field, low, high, kernel, bias, cot_own, cot_other,
               in_own, in_other, in_grad, after, out_own, out_other, grad, first, last, rim):
    half, starts = at[1], starts_of(at[0])
    for side, ref in ((0, low), (1, high)):
        for row in range(ref.shape[1]):
            for k, start in enumerate(starts):
                rim[side, row + 1 - half, pl.ds(start, 64), :] = ref[k, row]
        rim[side, 9 * half] = jnp.zeros(rim.shape[2:], BF16)
    for plane in range(2):
        out_own[plane + 1] = in_own[plane]
        out_other[plane + 1] = in_other[plane]
        grad[plane + 1] = in_grad[plane]

    def step(index, carry):
        row = 2 * index
        forward_rows(
            row, [(rim, 0), (field, 0), (field, 1)], kernel, bias,
            cot_own, cot_other, out_own, out_other, grad, 0, 0,
        )
        forward_rows(
            row, [(field, 2), (field, 3), (rim, 1)], kernel, bias,
            cot_own, cot_other, out_own, out_other, grad, 3, 3,
        )
        for r in range(2):
            first[row + r] = grad[0, row + r]
            last[row + r] = grad[3, row + r]
        return carry

    lax.fori_loop(0, 4, step, 0)


def spread(line):
    wide = line.astype(F32)
    return [moved(wide, c - 1).astype(BF16) for c in range(3)]


def weight_sums(at, planes, grad_of, cells_of, store, stacked):
    rows, outs = stacked.shape[1], stacked.shape[2] // 3
    for k in range(planes):
        for row in range(rows):
            for c, line in enumerate(spread(grad_of(k, row))):
                stacked[k, row, outs * c : outs * (c + 1), :] = line
    for a in range(3):

        def step(b, carry):
            total = jnp.zeros((3 * outs, 256), F32)
            for k in range(planes):
                grads = jnp.concatenate([stacked[k, row] for row in range(rows)], axis=1)
                ref, plane = cells_of(k, a)
                cells = jnp.concatenate([ref[plane, row + b] for row in range(rows)], axis=1)
                total = total + lax.dot_general(
                    grads, cells, (((1,), (1,)), ((), ())), preferred_element_type=F32
                )
            for c in range(3):
                line = pl.multiple_of(16 * (9 * a + 3 * b + c), 16)
                for side in range(2):
                    low = outs * c + 32 * side
                    parts = total[low : low + 16], total[low + 16 : low + 32]
                    kept = jnp.where(at[2] == 0, parts[0], parts[1])
                    given = jnp.where(at[2] == 0, parts[1], parts[0])
                    store(side ^ at[1], pl.ds(line, 16), kept, given)
            return carry

        lax.fori_loop(0, 3, step, 0)


def inner_weight_body(at, field, grad, kernel, keep, give, turned, turned_edge, stacked):
    width = kernel.shape[1]
    wide = [kernel[ab] for ab in range(9)]
    for k in range(0, 8, 2):
        turned[:, width * k : width * (k + 2)] = jnp.concatenate(wide[k : k + 2], axis=0).T
    turned[:, 8 * width :] = wide[8].T
    beside = [
        jnp.where(at[1] == 0, kernel[3 * a + 2], kernel[3 * a]) for a in range(3)
    ]
    turned_edge[...] = jnp.concatenate(beside, axis=0).T

    def store(side, lines, kept, given):
        keep[side, lines, :] = kept
        give[side, lines, :] = given

    weight_sums(
        at, 2, lambda k, row: grad[k, row], lambda k, a: (field, k + a), store, stacked
    )


def outer_weight_body(at, field, rim, grad, in_keep, in_give, after, keep, give, stacked):
    for side in range(2):
        for ref in (keep, give):
            ref[side, 432:448, :] = jnp.zeros((16, 256), F32)

    def store(side, lines, kept, given):
        keep[side, lines, :] = kept + in_keep[side, lines, :]
        give[side, lines, :] = given + in_give[side, lines, :]

    places = [[(rim, 0), (field, 0), (field, 1)], [(field, 2), (field, 3), (rim, 1)]]
    weight_sums(
        at, 2, lambda k, row: grad[3 * k, row], lambda k, a: places[k][a], store, stacked
    )


def input_terms(at, lines, planes, turned, turned_edge, outs, stacked, held):
    half, starts = at[1], starts_of(at[0])
    rows, width = 8, stacked.shape[2] // 3
    for plane, line_of in enumerate(lines):
        for row in range(rows):
            for c, value in enumerate(spread(line_of(row))):
                stacked[plane, row + 1, width * c : width * (c + 1), :] = value
        for row in (0, 9):
            stacked[plane, row] = jnp.zeros(stacked.shape[2:], BF16)

    def store(places):
        for start, ref in zip(starts, outs):
            block = held[pl.ds(start, 64), :]
            for r, (plane, row) in enumerate(places):
                ref[plane, row] = block[:, 128 * r : 128 * r + 128].astype(ref.dtype)

    def step(index, carry):
        row = 2 * index
        for first, plane in planes:
            terms = jnp.concatenate(
                [
                    pair_of(stacked, first + 2 - a, row + 2 - b)
                    for a in range(3)
                    for b in range(3)
                ],
                axis=0,
            )
            held[...] = jnp.dot(turned[...], terms, preferred_element_type=F32)
            store([(plane, row), (plane, row + 1)])
        return carry

    lax.fori_loop(0, rows // 2, step, 0)
    nearest = 8 - 7 * half
    terms = jnp.concatenate(
        [
            jnp.concatenate([stacked[first + 2 - a, nearest] for first, _ in planes], axis=1)
            for a in range(3)
        ],
        axis=0,
    )
    held[...] = jnp.dot(turned_edge[...], terms, preferred_element_type=F32)
    store([(plane, rows) for _, plane in planes])


def inner_input_body(at, grad, turned, turned_edge, after, own, near, far, back, stacked, held):
    lines = [lambda row, k=k: grad[k, row] for k in range(4)]
    input_terms(
        at, lines, [(0, 0), (1, 1)], turned, turned_edge, (own, near, far, back), stacked, held
    )


def outer_input_body(at, grad, low, high, turned, turned_edge, *refs):
    given, outs, (stacked, held) = refs[:4], refs[5:9], refs[9:]
    for source, ref in zip(given, outs):
        for plane in range(2):
            ref[plane + 1] = source[plane]
    lines = [lambda row, k=k: grad[k, row] for k in range(4)]
    lines = [lambda row: low[row]] + lines + [lambda row: high[row]]
    input_terms(at, lines, [(0, 0), (3, 3)], turned, turned_edge, outs, stacked, held)


def total_body(at, own, near, far, back, kept, sent):
    half = at[1]
    mine = pl.multiple_of(32 * half, 32)
    others = pl.multiple_of(32 * (1 - half), 32)

    def sums(plane, row, start):
        value = own[plane, row, pl.ds(start, 32), :]
        for ref in (near, far, back):
            value = value + ref[plane, row, pl.ds(start, 32), :].astype(F32)
        return value

    for plane in range(4):
        for row in range(9):
            kept[plane, row] = sums(plane, row, mine)
            sent[plane, row] = sums(plane, row, others).astype(BF16)


def join_body(at, kept, got, joined):
    half = at[1]
    for plane in range(4):
        for row in range(8):
            joined[plane, 8 * half + row] = kept[plane, row].astype(BF16)
            joined[plane, 8 - 8 * half + row] = got[plane, row]
        beside = 7 * (1 - half)
        joined[plane, 8 * half + beside] = (
            kept[plane, beside] + got[plane, 8].astype(F32)
        ).astype(BF16)
        beyond = 7 * half
        joined[plane, 8 - 8 * half + beyond] = (
            kept[plane, 8] + got[plane, beyond].astype(F32)
        ).astype(BF16)


def add_body(at, keep, got, first, second, third, chip):
    chip[...] = (keep[...] + got[...]).astype(BF16)


def mean_body(at, pieces, copies):
    total = pieces[0].astype(F32)
    for k in range(1, pieces.shape[0]):
        total = total + pieces[k].astype(F32)
    total = total * (1.0 / math.sqrt(64 * 16 * 128))
    for k in range(copies.shape[0]):
        copies[k] = total


def weave_body(at, mine, other, joined):
    core = at[2]
    for tap in range(27):
        first, second = (ref[16 * tap : 16 * tap + 16] for ref in (mine, other))
        joined[tap, :16] = jnp.where(core == 0, first, second)
        joined[tap, 16:] = jnp.where(core == 0, second, first)


def call(body, n_in, outs, scratch, flops, after=0):
    vmem = pl.BlockSpec(memory_space=pltpu.VMEM)
    anywhere = pl.BlockSpec(memory_space=pl.ANY)
    return pl.pallas_call(
        body,
        out_shape=[jax.ShapeDtypeStruct(*out) for out in outs],
        in_specs=[pl.BlockSpec(memory_space=pltpu.SMEM)]
        + [vmem] * (n_in - 1)
        + [anywhere] * after,
        out_specs=[vmem] * len(outs),
        scratch_shapes=scratch,
        compiler_params=pltpu.CompilerParams(vmem_limit_bytes=VMEM_LIMIT),
        cost_estimate=pl.CostEstimate(
            flops=flops, bytes_accessed=8 * 2**20, transcendentals=2**18
        ),
    )


def on_device(volume, kernel, bias, cotangent):
    here_y, half, core = lax.axis_index("y"), lax.axis_index("xh"), lax.axis_index("core")
    at = jnp.stack([here_y, half, core]).astype(jnp.int32)

    def swap(value):
        return lax.ppermute(value, "xh", [(0, 1), (1, 0)])

    def swap_core(value):
        return lax.ppermute(value, "core", [(0, 1), (1, 0)])

    def turn(value, step):
        return lax.ppermute(value, "y", [(i, (i + step) % 4) for i in range(4)])

    def up(value):
        return lax.ppermute(value, SPACE, [(i, i + 1) for i in range(15)])

    def down(value):
        return lax.ppermute(value, SPACE, [(i + 1, i) for i in range(15)])

    mine = lax.dynamic_slice_in_dim(volume, 7 * half, 9, axis=1)
    got = swap(lax.dynamic_slice_in_dim(volume, 7 * (1 - half), 9, axis=1))
    own_lo, own_hi = (
        jnp.where(
            half == 0,
            jnp.concatenate([mine[k : k + 2], got[k : k + 2]], axis=2),
            jnp.concatenate([got[k : k + 2], mine[k : k + 2]], axis=2),
        )
        for k in (0, 2)
    )
    left_lo, right_hi = turn(own_lo, 1), turn(own_hi, -1)
    left_hi, right_lo = turn(own_hi, 1), turn(own_lo, -1)
    far_lo, far_hi = turn(left_lo, 1), turn(right_hi, -1)
    kernel_sent, cot_own, cot_sent = call(
        ready_body, 4,
        [((29, 32, 256), BF16), ((4, 8, 32, 128), BF16), ((4, 8, 32, 128), BF16)],
        [], 10**6, 1,
    )(at, kernel, jnp.broadcast_to(bias[:, None], (32, 128)), cotangent, own_lo)
    kernel_other, cot_other = swap(kernel_sent), swap(cot_sent)
    up_rim, down_rim = call(rims_body, 9, [((4, 9, 64, 128), BF16)] * 2, [], 10**6, 2)(
        at, own_lo, own_hi, left_lo, left_hi, right_lo, right_hi, far_lo, far_hi,
        kernel_other, cot_other,
    )
    low, high = up(up_rim), down(down_rim)

    flops = 36 * 10**8
    out_own, out_other, grad, field, taps, bias_wide = call(
        inner_body, 13,
        [
            ((2, 8, 32, 128), BF16), ((2, 8, 32, 128), BF16), ((2, 8, 64, 128), BF16),
            ((4, 10, 256, 128), BF16), ((9, 192, 256), BF16),
            ((64, 128), F32),
        ],
        [], flops // 2,
    )(at, own_lo, own_hi, left_lo, left_hi, right_lo, right_hi, far_lo, far_hi,
      kernel_sent, kernel_other, cot_own, cot_other)
    keep, give, turned, turned_edge = call(
        inner_weight_body, 4,
        [((2, 448, 256), F32)] * 2 + [((256, 1728), BF16), ((256, 576), BF16)],
        [pltpu.VMEM((2, 8, 192, 128), BF16)], flops // 2,
    )(at, field, grad, taps)
    out_own, out_other, grad, first, last, rim = call(
        outer_body, 11,
        [
            ((4, 8, 32, 128), BF16), ((4, 8, 32, 128), BF16), ((4, 8, 64, 128), BF16),
            ((8, 64, 128), BF16), ((8, 64, 128), BF16), ((2, 10, 256, 128), BF16),
        ],
        [], flops // 2, 1,
    )(at, field, low, high, taps, bias_wide, cot_own, cot_other,
      out_own, out_other, grad, keep)

    got_out = swap(out_other)
    output = jnp.where(
        half == 0,
        jnp.concatenate([out_own, got_out], axis=1),
        jnp.concatenate([got_out, out_own], axis=1),
    )
    grad_low, grad_high = up(last), down(first)

    def input_chunk(chunk, rim):
        return call(
            functools.partial(input_body, chunk), 5,
            [((2, 9, 64, 128), F32)] + [((2, 9, 64, 128), BF16)] * 3,
            [pltpu.VMEM((4, 10, 192, 128), BF16), pltpu.VMEM((256, 256), F32)],
            flops // 2,
        )(at, grad, rim, turned, turned_edge)

    def input_shapes(planes):
        return [((planes, 9, 64, 128), F32)] + [((planes, 9, 64, 128), BF16)] * 3

    def input_scratch(planes):
        return [pltpu.VMEM((planes, 10, 192, 128), BF16), pltpu.VMEM((256, 256), F32)]

    keep, give = call(
        outer_weight_body, 6, [((2, 448, 256), F32)] * 2,
        [pltpu.VMEM((2, 8, 192, 128), BF16)], flops // 2, 1,
    )(at, field, rim, grad, keep, give, grad)
    parts = call(
        inner_input_body, 4, input_shapes(2), input_scratch(4), flops // 2, 1
    )(at, grad, turned, turned_edge, keep)
    own, near, far, back = call(
        outer_input_body, 10, input_shapes(4), input_scratch(6), flops // 2, 1
    )(at, grad, grad_low, grad_high, turned, turned_edge, *parts, keep)
    (chip,) = call(add_body, 3, [((2, 448, 256), BF16)], [], 10**6, 3)(
        at, keep, swap_core(give), near, near, near
    )
    pieces = lax.all_to_all(
        chip.reshape(16, 56, 256), ("xh", "z", "xl"), 0, 0, tiled=True
    )
    near, back, far = turn(near, 1), turn(back, -1), turn(far, 2)
    kept, sent = call(
        total_body, 5, [((4, 9, 32, 128), F32), ((4, 9, 32, 128), BF16)], [], 10**6
    )(at, own, near, far, back)
    got = swap(sent)
    (copies,) = call(mean_body, 2, [((8, 56, 256), F32)], [], 10**6)(at, pieces)
    everyone = lax.all_to_all(copies, ("z", "xl"), 0, 0, tiled=True).reshape(448, 256)
    (weight_grad,) = call(weave_body, 3, [((27, 32, 256), F32)], [], 10**6)(
        at, everyone, swap_core(everyone)
    )
    (input_grad,) = call(join_body, 3, [((4, 16, 32, 128), BF16)], [], 10**6)(at, kept, got)
    return output, input_grad, weight_grad


def solution(mesh):
    split = Mesh(mesh.devices.reshape(4, 2, 4, 2, 2), CHAN + SPACE)
    return jax.shard_map(
        on_device,
        mesh=split,
        in_specs=(
            P(SPACE, None, CHAN, None),
            P(None, CHAN, None),
            P(CHAN),
            P(SPACE, None, CHAN, None),
        ),
        out_specs=(
            P(SPACE, None, CHAN, None),
            P(SPACE, None, CHAN, None),
            P(None, CHAN, None),
        ),
        check_vma=False,
    )
```

```python
import functools
import math

import jax
import jax.numpy as jnp
from jax import lax
from jax.experimental import pallas as pl
from jax.experimental.pallas import tpu as pltpu
from jax.sharding import Mesh
from jax.sharding import PartitionSpec as P

BF16 = jnp.bfloat16
F32 = jnp.float32
VMEM_LIMIT = 20 * 1024 * 1024
CHAN = ("y", "xh")
SPACE = ("z", "xl", "core")


def moved(value, step):
    if step == 0:
        return value
    size = value.shape[-1]
    lane = lax.broadcasted_iota(jnp.int32, value.shape, value.ndim - 1)
    rolled = pltpu.roll(value, step % size, value.ndim - 1)
    edge = 0 if step == 1 else size - 1
    return jnp.where(lane == edge, 0.0, rolled)


def pair_of(ref, plane, row):
    return jnp.concatenate([ref[plane, row], ref[plane, row + 1]], axis=1)


def starts_of(here_y):
    return [pl.multiple_of(lax.rem(here_y + shift, 4) * 64, 64) for shift in range(4)]


def forward_rows(row, places, kernel, bias, cot_own, cot_other, out_own, out_other, grad,
                 plane_cot, plane_out):
    outs = kernel.shape[1] // 3
    total = jnp.zeros((3 * outs, 256), F32)
    for a, (ref, plane) in enumerate(places):
        for b in range(3):
            total = total + jnp.dot(
                kernel[3 * a + b], pair_of(ref, plane, row + b), preferred_element_type=F32
            )
    others = cot_other[29 + 4 * plane_cot + row // 2]
    for r in range(2):
        part = total[:, 128 * r : 128 * r + 128]
        pre = (
            moved(part[:outs], 1) + part[outs : 2 * outs] + moved(part[2 * outs :], -1)
            + bias[...]
        )
        sig = 1.0 / (1.0 + jnp.exp(-pre))
        out = (pre * sig).astype(BF16)
        out_own[plane_out, row + r] = out[: outs // 2]
        out_other[plane_out, row + r] = out[outs // 2 :]
        cot = jnp.concatenate(
            [cot_own[plane_cot, row + r], others[:, 128 * r : 128 * r + 128]], axis=0
        ).astype(F32)
        grad[plane_out, row + r] = (cot * sig * (1.0 + pre * (1.0 - sig))).astype(BF16)


def ready_body(at, kernel, bias, cotangent, after, kernel_out, cot_own):
    half = at[1]
    kernel_out[:27] = kernel[...]
    rest = bias[...]
    for k in range(3):
        part = rest.astype(BF16)
        kernel_out[27 + k // 2, :, 128 * (k % 2) : 128 * (k % 2) + 128] = part
        rest = rest - part.astype(F32)
    kernel_out[28, :, 128:] = jnp.zeros((32, 128), BF16)
    for plane in range(4):
        for row in range(8):
            cot_own[plane, row] = cotangent[plane, 8 * half + row]
            place, low = 29 + 4 * plane + row // 2, 128 * (row % 2)
            kernel_out[place, :, low : low + 128] = cotangent[plane, 8 - 8 * half + row]


def rims_body(at, own_lo, own_hi, left_lo, left_hi, right_lo, right_hi, far_lo, far_hi,
              kernel, up_rim, down_rim):
    for k, (lower, upper) in enumerate(
        ((own_lo, own_hi), (right_lo, right_hi), (far_lo, far_hi), (left_lo, left_hi))
    ):
        up_rim[k] = upper[1]
        down_rim[k] = lower[0]


def inner_body(at, own_lo, own_hi, left_lo, left_hi, right_lo, right_hi, far_lo, far_hi,
               kernel_own, kernel_other, cot_own, out_own, out_other, grad,
               field, kernel, bias):
    half, starts = at[1], starts_of(at[0])
    rows = own_lo.shape[1]

    def fill_kernel(ab, carry):
        for c in range(3):
            kernel[ab, 64 * c : 64 * c + 32] = kernel_own[3 * ab + c]
            kernel[ab, 64 * c + 32 : 64 * c + 64] = kernel_other[3 * ab + c]
        return carry

    lax.fori_loop(0, 9, fill_kernel, 0)
    for k, ref in enumerate((kernel_own, kernel_other)):
        bias[32 * k : 32 * k + 32] = (
            ref[27, :, :128].astype(F32) + ref[27, :, 128:].astype(F32)
        ) + ref[28, :, :128].astype(F32)
    sources = (own_lo, own_hi), (right_lo, right_hi), (far_lo, far_hi), (left_lo, left_hi)

    def fill(k, carry):
        for upper in range(2):
            plane = k + 2 * upper
            for row in range(rows):
                for start, pair in zip(starts, sources):
                    field[plane, row + 1 - half, pl.ds(start, 64), :] = pair[upper][k, row]
            field[plane, 9 * half] = jnp.zeros(field.shape[2:], BF16)
        return carry

    lax.fori_loop(0, 2, fill, 0)

    def step(index, carry):
        plane, row = index // 4, 2 * lax.rem(index, 4)
        forward_rows(
            row, [(field, plane), (field, plane + 1), (field, plane + 2)], kernel, bias,
            cot_own, kernel_other, out_own, out_other, grad, plane + 1, plane,
        )
        return carry

    lax.fori_loop(0, 8, step, 0)


def outer_body(at, field, low, high, kernel, bias, cot_own, cot_other,
               in_own, in_other, in_grad, after, out_own, out_other, grad, first, last, rim):
    half, starts = at[1], starts_of(at[0])
    for side, ref in ((0, low), (1, high)):
        for row in range(ref.shape[1]):
            for k, start in enumerate(starts):
                rim[side, row + 1 - half, pl.ds(start, 64), :] = ref[k, row]
        rim[side, 9 * half] = jnp.zeros(rim.shape[2:], BF16)
    for plane in range(2):
        out_own[plane + 1] = in_own[plane]
        out_other[plane + 1] = in_other[plane]
        grad[plane + 1] = in_grad[plane]

    def step(index, carry):
        row = 2 * index
        forward_rows(
            row, [(rim, 0), (field, 0), (field, 1)], kernel, bias,
            cot_own, cot_other, out_own, out_other, grad, 0, 0,
        )
        forward_rows(
            row, [(field, 2), (field, 3), (rim, 1)], kernel, bias,
            cot_own, cot_other, out_own, out_other, grad, 3, 3,
        )
        for r in range(2):
            first[row + r] = grad[0, row + r]
            last[row + r] = grad[3, row + r]
        return carry

    lax.fori_loop(0, 4, step, 0)


def spread(line):
    wide = line.astype(F32)
    return [moved(wide, c - 1).astype(BF16) for c in range(3)]


def weight_sums(at, planes, grad_of, cells_of, store, stacked):
    rows, outs = stacked.shape[1], stacked.shape[2] // 3
    for k in range(planes):
        for row in range(rows):
            for c, line in enumerate(spread(grad_of(k, row))):
                stacked[k, row, outs * c : outs * (c + 1), :] = line
    for a in range(3):

        def step(b, carry):
            total = jnp.zeros((3 * outs, 256), F32)
            for k in range(planes):
                grads = jnp.concatenate([stacked[k, row] for row in range(rows)], axis=1)
                ref, plane = cells_of(k, a)
                cells = jnp.concatenate([ref[plane, row + b] for row in range(rows)], axis=1)
                total = total + lax.dot_general(
                    grads, cells, (((1,), (1,)), ((), ())), preferred_element_type=F32
                )
            for c in range(3):
                line = pl.multiple_of(16 * (9 * a + 3 * b + c), 16)
                for side in range(2):
                    low = outs * c + 32 * side
                    parts = total[low : low + 16], total[low + 16 : low + 32]
                    kept = jnp.where(at[2] == 0, parts[0], parts[1])
                    given = jnp.where(at[2] == 0, parts[1], parts[0])
                    store(side ^ at[1], pl.ds(line, 16), kept, given)
            return carry

        lax.fori_loop(0, 3, step, 0)


def inner_weight_body(at, field, grad, kernel, keep, give, turned, turned_edge, stacked):
    width = kernel.shape[1]
    wide = [kernel[ab] for ab in range(9)]
    for k in range(0, 8, 2):
        turned[:, width * k : width * (k + 2)] = jnp.concatenate(wide[k : k + 2], axis=0).T
    turned[:, 8 * width :] = wide[8].T
    beside = [
        jnp.where(at[1] == 0, kernel[3 * a + 2], kernel[3 * a]) for a in range(3)
    ]
    turned_edge[...] = jnp.concatenate(beside, axis=0).T

    def store(side, lines, kept, given):
        keep[side, lines, :] = kept
        give[side, lines, :] = given

    weight_sums(
        at, 2, lambda k, row: grad[k, row], lambda k, a: (field, k + a), store, stacked
    )


def outer_weight_body(at, field, rim, grad, in_keep, in_give, after, keep, give, stacked):
    for side in range(2):
        for ref in (keep, give):
            ref[side, 432:448, :] = jnp.zeros((16, 256), F32)

    def store(side, lines, kept, given):
        keep[side, lines, :] = kept + in_keep[side, lines, :]
        give[side, lines, :] = given + in_give[side, lines, :]

    places = [[(rim, 0), (field, 0), (field, 1)], [(field, 2), (field, 3), (rim, 1)]]
    weight_sums(
        at, 2, lambda k, row: grad[3 * k, row], lambda k, a: places[k][a], store, stacked
    )


def input_terms(at, lines, planes, turned, turned_edge, outs, stacked, held):
    half, starts = at[1], starts_of(at[0])
    rows, width = 8, stacked.shape[2] // 3
    for plane, line_of in enumerate(lines):
        for row in range(rows):
            for c, value in enumerate(spread(line_of(row))):
                stacked[plane, row + 1, width * c : width * (c + 1), :] = value
        for row in (0, 9):
            stacked[plane, row] = jnp.zeros(stacked.shape[2:], BF16)

    def store(places):
        for start, ref in zip(starts, outs):
            block = held[pl.ds(start, 64), :]
            for r, (plane, row) in enumerate(places):
                ref[plane, row] = block[:, 128 * r : 128 * r + 128].astype(ref.dtype)

    def step(index, carry):
        row = 2 * index
        for first, plane in planes:
            terms = jnp.concatenate(
                [
                    pair_of(stacked, first + 2 - a, row + 2 - b)
                    for a in range(3)
                    for b in range(3)
                ],
                axis=0,
            )
            held[...] = jnp.dot(turned[...], terms, preferred_element_type=F32)
            store([(plane, row), (plane, row + 1)])
        return carry

    lax.fori_loop(0, rows // 2, step, 0)
    nearest = 8 - 7 * half
    terms = jnp.concatenate(
        [
            jnp.concatenate([stacked[first + 2 - a, nearest] for first, _ in planes], axis=1)
            for a in range(3)
        ],
        axis=0,
    )
    held[...] = jnp.dot(turned_edge[...], terms, preferred_element_type=F32)
    store([(plane, rows) for _, plane in planes])


def inner_input_body(at, grad, turned, turned_edge, after, own, near, far, back, stacked, held):
    lines = [lambda row, k=k: grad[k, row] for k in range(4)]
    input_terms(
        at, lines, [(0, 0), (1, 1)], turned, turned_edge, (own, near, far, back), stacked, held
    )


def outer_input_body(at, grad, low, high, turned, turned_edge, *refs):
    given, outs, (stacked, held) = refs[:4], refs[5:9], refs[9:]
    for source, ref in zip(given, outs):
        for plane in range(2):
            ref[plane + 1] = source[plane]
    lines = [lambda row, k=k: grad[k, row] for k in range(4)]
    lines = [lambda row: low[row]] + lines + [lambda row: high[row]]
    input_terms(at, lines, [(0, 0), (3, 3)], turned, turned_edge, outs, stacked, held)


def total_body(at, own, near, far, back, kept, sent):
    half = at[1]
    mine = pl.multiple_of(32 * half, 32)
    others = pl.multiple_of(32 * (1 - half), 32)

    def sums(plane, row, start):
        value = own[plane, row, pl.ds(start, 32), :]
        for ref in (near, far, back):
            value = value + ref[plane, row, pl.ds(start, 32), :].astype(F32)
        return value

    for plane in range(4):
        for row in range(9):
            kept[plane, row] = sums(plane, row, mine)
            sent[plane, row] = sums(plane, row, others).astype(BF16)


def join_body(at, kept, got, joined):
    half = at[1]
    for plane in range(4):
        for row in range(8):
            joined[plane, 8 * half + row] = kept[plane, row].astype(BF16)
            joined[plane, 8 - 8 * half + row] = got[plane, row]
        beside = 7 * (1 - half)
        joined[plane, 8 * half + beside] = (
            kept[plane, beside] + got[plane, 8].astype(F32)
        ).astype(BF16)
        beyond = 7 * half
        joined[plane, 8 - 8 * half + beyond] = (
            kept[plane, 8] + got[plane, beyond].astype(F32)
        ).astype(BF16)


def add_body(at, keep, got, first, second, third, chip):
    chip[...] = (keep[...] + got[...]).astype(BF16)


def mean_body(at, pieces, copies):
    total = pieces[0].astype(F32)
    for k in range(1, pieces.shape[0]):
        total = total + pieces[k].astype(F32)
    total = total * (1.0 / math.sqrt(64 * 16 * 128))
    for k in range(copies.shape[0]):
        copies[k] = total


def weave_body(at, mine, other, joined):
    core = at[2]
    for tap in range(27):
        first, second = (ref[16 * tap : 16 * tap + 16] for ref in (mine, other))
        joined[tap, :16] = jnp.where(core == 0, first, second)
        joined[tap, 16:] = jnp.where(core == 0, second, first)


def call(body, n_in, outs, scratch, flops, after=0):
    vmem = pl.BlockSpec(memory_space=pltpu.VMEM)
    anywhere = pl.BlockSpec(memory_space=pl.ANY)
    return pl.pallas_call(
        body,
        out_shape=[jax.ShapeDtypeStruct(*out) for out in outs],
        in_specs=[pl.BlockSpec(memory_space=pltpu.SMEM)]
        + [vmem] * (n_in - 1)
        + [anywhere] * after,
        out_specs=[vmem] * len(outs),
        scratch_shapes=scratch,
        compiler_params=pltpu.CompilerParams(vmem_limit_bytes=VMEM_LIMIT),
        cost_estimate=pl.CostEstimate(
            flops=flops, bytes_accessed=8 * 2**20, transcendentals=2**18
        ),
    )


def on_device(volume, kernel, bias, cotangent):
    here_y, half, core = lax.axis_index("y"), lax.axis_index("xh"), lax.axis_index("core")
    at = jnp.stack([here_y, half, core]).astype(jnp.int32)

    def swap(value):
        return lax.ppermute(value, "xh", [(0, 1), (1, 0)])

    def swap_core(value):
        return lax.ppermute(value, "core", [(0, 1), (1, 0)])

    def turn(value, step):
        return lax.ppermute(value, "y", [(i, (i + step) % 4) for i in range(4)])

    def up(value):
        return lax.ppermute(value, SPACE, [(i, i + 1) for i in range(15)])

    def down(value):
        return lax.ppermute(value, SPACE, [(i + 1, i) for i in range(15)])

    mine = lax.dynamic_slice_in_dim(volume, 7 * half, 9, axis=1)
    got = swap(lax.dynamic_slice_in_dim(volume, 7 * (1 - half), 9, axis=1))
    own_lo, own_hi = (
        jnp.where(
            half == 0,
            jnp.concatenate([mine[k : k + 2], got[k : k + 2]], axis=2),
            jnp.concatenate([got[k : k + 2], mine[k : k + 2]], axis=2),
        )
        for k in (0, 2)
    )
    left_lo, right_hi = turn(own_lo, 1), turn(own_hi, -1)
    left_hi, right_lo = turn(own_hi, 1), turn(own_lo, -1)
    far_lo, far_hi = turn(left_lo, 1), turn(right_hi, -1)
    kernel_sent, cot_own = call(
        ready_body, 4, [((45, 32, 256), BF16), ((4, 8, 32, 128), BF16)],
        [], 10**6, 1,
    )(at, kernel, jnp.broadcast_to(bias[:, None], (32, 128)), cotangent, own_lo)
    kernel_other = swap(kernel_sent)
    up_rim, down_rim = call(rims_body, 9, [((4, 9, 64, 128), BF16)] * 2, [], 10**6, 1)(
        at, own_lo, own_hi, left_lo, left_hi, right_lo, right_hi, far_lo, far_hi,
        kernel_other,
    )
    low, high = up(up_rim), down(down_rim)

    flops = 36 * 10**8
    out_own, out_other, grad, field, taps, bias_wide = call(
        inner_body, 12,
        [
            ((2, 8, 32, 128), BF16), ((2, 8, 32, 128), BF16), ((2, 8, 64, 128), BF16),
            ((4, 10, 256, 128), BF16), ((9, 192, 256), BF16),
            ((64, 128), F32),
        ],
        [], flops // 2,
    )(at, own_lo, own_hi, left_lo, left_hi, right_lo, right_hi, far_lo, far_hi,
      kernel_sent, kernel_other, cot_own)
    keep, give, turned, turned_edge = call(
        inner_weight_body, 4,
        [((2, 448, 256), F32)] * 2 + [((256, 1728), BF16), ((256, 576), BF16)],
        [pltpu.VMEM((2, 8, 192, 128), BF16)], flops // 2,
    )(at, field, grad, taps)
    out_own, out_other, grad, first, last, rim = call(
        outer_body, 11,
        [
            ((4, 8, 32, 128), BF16), ((4, 8, 32, 128), BF16), ((4, 8, 64, 128), BF16),
            ((8, 64, 128), BF16), ((8, 64, 128), BF16), ((2, 10, 256, 128), BF16),
        ],
        [], flops // 2, 1,
    )(at, field, low, high, taps, bias_wide, cot_own, kernel_other,
      out_own, out_other, grad, keep)

    got_out = swap(out_other)
    output = jnp.where(
        half == 0,
        jnp.concatenate([out_own, got_out], axis=1),
        jnp.concatenate([got_out, out_own], axis=1),
    )
    grad_low, grad_high = up(last), down(first)

    def input_chunk(chunk, rim):
        return call(
            functools.partial(input_body, chunk), 5,
            [((2, 9, 64, 128), F32)] + [((2, 9, 64, 128), BF16)] * 3,
            [pltpu.VMEM((4, 10, 192, 128), BF16), pltpu.VMEM((256, 256), F32)],
            flops // 2,
        )(at, grad, rim, turned, turned_edge)

    def input_shapes(planes):
        return [((planes, 9, 64, 128), F32)] + [((planes, 9, 64, 128), BF16)] * 3

    def input_scratch(planes):
        return [pltpu.VMEM((planes, 10, 192, 128), BF16), pltpu.VMEM((256, 256), F32)]

    keep, give = call(
        outer_weight_body, 6, [((2, 448, 256), F32)] * 2,
        [pltpu.VMEM((2, 8, 192, 128), BF16)], flops // 2, 1,
    )(at, field, rim, grad, keep, give, grad)
    parts = call(
        inner_input_body, 4, input_shapes(2), input_scratch(4), flops // 2, 1
    )(at, grad, turned, turned_edge, keep)
    own, near, far, back = call(
        outer_input_body, 10, input_shapes(4), input_scratch(6), flops // 2, 1
    )(at, grad, grad_low, grad_high, turned, turned_edge, *parts, keep)
    (chip,) = call(add_body, 3, [((2, 448, 256), BF16)], [], 10**6, 3)(
        at, keep, swap_core(give), near, near, near
    )
    pieces = lax.all_to_all(
        chip.reshape(16, 56, 256), ("xh", "z", "xl"), 0, 0, tiled=True
    )
    near, back, far = turn(near, 1), turn(back, -1), turn(far, 2)
    kept, sent = call(
        total_body, 5, [((4, 9, 32, 128), F32), ((4, 9, 32, 128), BF16)], [], 10**6
    )(at, own, near, far, back)
    got = swap(sent)
    (copies,) = call(mean_body, 2, [((8, 56, 256), F32)], [], 10**6)(at, pieces)
    everyone = lax.all_to_all(copies, ("z", "xl"), 0, 0, tiled=True).reshape(448, 256)
    (weight_grad,) = call(weave_body, 3, [((27, 32, 256), F32)], [], 10**6)(
        at, everyone, swap_core(everyone)
    )
    (input_grad,) = call(join_body, 3, [((4, 16, 32, 128), BF16)], [], 10**6)(at, kept, got)
    return output, input_grad, weight_grad


def solution(mesh):
    split = Mesh(mesh.devices.reshape(4, 2, 4, 2, 2), CHAN + SPACE)
    return jax.shard_map(
        on_device,
        mesh=split,
        in_specs=(
            P(SPACE, None, CHAN, None),
            P(None, CHAN, None),
            P(CHAN),
            P(SPACE, None, CHAN, None),
        ),
        out_specs=(
            P(SPACE, None, CHAN, None),
            P(SPACE, None, CHAN, None),
            P(None, CHAN, None),
        ),
        check_vma=False,
    )
```

```python
import functools
import math

import jax
import jax.numpy as jnp
from jax import lax
from jax.experimental import pallas as pl
from jax.experimental.pallas import tpu as pltpu
from jax.sharding import Mesh
from jax.sharding import PartitionSpec as P

BF16 = jnp.bfloat16
F32 = jnp.float32
VMEM_LIMIT = 20 * 1024 * 1024
CHAN = ("y", "xh")
SPACE = ("z", "xl", "core")


def moved(value, step):
    if step == 0:
        return value
    size = value.shape[-1]
    lane = lax.broadcasted_iota(jnp.int32, value.shape, value.ndim - 1)
    rolled = pltpu.roll(value, step % size, value.ndim - 1)
    edge = 0 if step == 1 else size - 1
    return jnp.where(lane == edge, 0.0, rolled)


def pair_of(ref, plane, row):
    return jnp.concatenate([ref[plane, row], ref[plane, row + 1]], axis=1)


def starts_of(here_y):
    return [pl.multiple_of(lax.rem(here_y + shift, 4) * 64, 64) for shift in range(4)]


def forward_rows(row, places, kernel, bias, cot_own, cot_other, out_own, out_other, grad,
                 plane_cot, plane_out):
    outs = kernel.shape[1] // 3
    total = jnp.zeros((3 * outs, 256), F32)
    for a, (ref, plane) in enumerate(places):
        for b in range(3):
            total = total + jnp.dot(
                kernel[3 * a + b], pair_of(ref, plane, row + b), preferred_element_type=F32
            )
    others = cot_other[29 + 4 * plane_cot + row // 2]
    for r in range(2):
        part = total[:, 128 * r : 128 * r + 128]
        pre = (
            moved(part[:outs], 1) + part[outs : 2 * outs] + moved(part[2 * outs :], -1)
            + bias[...]
        )
        sig = 1.0 / (1.0 + jnp.exp(-pre))
        out = (pre * sig).astype(BF16)
        out_own[plane_out, row + r] = out[: outs // 2]
        out_other[plane_out, row + r] = out[outs // 2 :]
        cot = jnp.concatenate(
            [cot_own[plane_cot, row + r], others[:, 128 * r : 128 * r + 128]], axis=0
        ).astype(F32)
        grad[plane_out, row + r] = (cot * sig * (1.0 + pre * (1.0 - sig))).astype(BF16)


def ready_body(at, kernel, bias, cotangent, after, kernel_out, cot_own):
    half = at[1]
    kernel_out[:27] = kernel[...]
    rest = bias[...]
    for k in range(3):
        part = rest.astype(BF16)
        kernel_out[27 + k // 2, :, 128 * (k % 2) : 128 * (k % 2) + 128] = part
        rest = rest - part.astype(F32)
    kernel_out[28, :, 128:] = jnp.zeros((32, 128), BF16)
    for plane in range(4):
        for row in range(8):
            cot_own[plane, row] = cotangent[plane, 8 * half + row]
            place, low = 29 + 4 * plane + row // 2, 128 * (row % 2)
            kernel_out[place, :, low : low + 128] = cotangent[plane, 8 - 8 * half + row]


def rims_body(at, own_lo, own_hi, left_lo, left_hi, right_lo, right_hi, far_lo, far_hi,
              kernel, up_rim, down_rim):
    for k, (lower, upper) in enumerate(
        ((own_lo, own_hi), (right_lo, right_hi), (far_lo, far_hi), (left_lo, left_hi))
    ):
        up_rim[k] = upper[1]
        down_rim[k] = lower[0]


def inner_body(at, own_lo, own_hi, left_lo, left_hi, right_lo, right_hi, far_lo, far_hi,
               kernel_own, kernel_other, cot_own, out_own, out_other, grad,
               field, kernel, bias):
    half, starts = at[1], starts_of(at[0])
    rows = own_lo.shape[1]

    def fill_kernel(ab, carry):
        for c in range(3):
            kernel[ab, 64 * c : 64 * c + 32] = kernel_own[3 * ab + c]
            kernel[ab, 64 * c + 32 : 64 * c + 64] = kernel_other[3 * ab + c]
        return carry

    lax.fori_loop(0, 9, fill_kernel, 0)
    for k, ref in enumerate((kernel_own, kernel_other)):
        bias[32 * k : 32 * k + 32] = (
            ref[27, :, :128].astype(F32) + ref[27, :, 128:].astype(F32)
        ) + ref[28, :, :128].astype(F32)
    sources = (own_lo, own_hi), (right_lo, right_hi), (far_lo, far_hi), (left_lo, left_hi)

    def fill(k, carry):
        for upper in range(2):
            plane = k + 2 * upper
            for row in range(rows):
                for start, pair in zip(starts, sources):
                    field[plane, row + 1 - half, pl.ds(start, 64), :] = pair[upper][k, row]
            field[plane, 9 * half] = jnp.zeros(field.shape[2:], BF16)
        return carry

    lax.fori_loop(0, 2, fill, 0)

    def step(index, carry):
        plane, row = index // 4, 2 * lax.rem(index, 4)
        forward_rows(
            row, [(field, plane), (field, plane + 1), (field, plane + 2)], kernel, bias,
            cot_own, kernel_other, out_own, out_other, grad, plane + 1, plane,
        )
        return carry

    lax.fori_loop(0, 8, step, 0)


def outer_body(at, field, low, high, kernel, bias, cot_own, cot_other,
               in_own, in_other, in_grad, after, out_own, out_other, grad, first, last, rim):
    half, starts = at[1], starts_of(at[0])
    for side, ref in ((0, low), (1, high)):
        for row in range(ref.shape[1]):
            for k, start in enumerate(starts):
                rim[side, row + 1 - half, pl.ds(start, 64), :] = ref[k, row]
        rim[side, 9 * half] = jnp.zeros(rim.shape[2:], BF16)
    for plane in range(2):
        out_own[plane + 1] = in_own[plane]
        out_other[plane + 1] = in_other[plane]
        grad[plane + 1] = in_grad[plane]

    def step(index, carry):
        row = 2 * index
        forward_rows(
            row, [(rim, 0), (field, 0), (field, 1)], kernel, bias,
            cot_own, cot_other, out_own, out_other, grad, 0, 0,
        )
        forward_rows(
            row, [(field, 2), (field, 3), (rim, 1)], kernel, bias,
            cot_own, cot_other, out_own, out_other, grad, 3, 3,
        )
        for r in range(2):
            first[row + r] = grad[0, row + r]
            last[row + r] = grad[3, row + r]
        return carry

    lax.fori_loop(0, 4, step, 0)


def spread(line):
    wide = line.astype(F32)
    return [moved(wide, c - 1).astype(BF16) for c in range(3)]


def weight_sums(at, planes, grad_of, cells_of, store, stacked):
    rows, outs = stacked.shape[1], stacked.shape[2] // 3
    for k in range(planes):
        for row in range(rows):
            for c, line in enumerate(spread(grad_of(k, row))):
                stacked[k, row, outs * c : outs * (c + 1), :] = line
    for a in range(3):

        def step(b, carry):
            total = jnp.zeros((256, 3 * outs), F32)
            for k in range(planes):
                grads = jnp.concatenate([stacked[k, row] for row in range(rows)], axis=1)
                ref, plane = cells_of(k, a)
                cells = jnp.concatenate([ref[plane, row + b] for row in range(rows)], axis=1)
                total = total + lax.dot_general(
                    cells, grads, (((1,), (1,)), ((), ())), preferred_element_type=F32
                )
            total = total.T
            for c in range(3):
                line = pl.multiple_of(16 * (9 * a + 3 * b + c), 16)
                for side in range(2):
                    low = outs * c + 32 * side
                    parts = total[low : low + 16], total[low + 16 : low + 32]
                    kept = jnp.where(at[2] == 0, parts[0], parts[1])
                    given = jnp.where(at[2] == 0, parts[1], parts[0])
                    store(side ^ at[1], pl.ds(line, 16), kept, given)
            return carry

        lax.fori_loop(0, 3, step, 0)


def inner_weight_body(at, field, grad, kernel, keep, give, turned, turned_edge, stacked):
    width = kernel.shape[1]
    wide = [kernel[ab] for ab in range(9)]
    for k in range(0, 8, 2):
        turned[:, width * k : width * (k + 2)] = jnp.concatenate(wide[k : k + 2], axis=0).T
    turned[:, 8 * width :] = wide[8].T
    beside = [
        jnp.where(at[1] == 0, kernel[3 * a + 2], kernel[3 * a]) for a in range(3)
    ]
    turned_edge[...] = jnp.concatenate(beside, axis=0).T

    def store(side, lines, kept, given):
        keep[side, lines, :] = kept
        give[side, lines, :] = given

    weight_sums(
        at, 2, lambda k, row: grad[k, row], lambda k, a: (field, k + a), store, stacked
    )


def outer_weight_body(at, field, rim, grad, in_keep, in_give, after, keep, give, stacked):
    for side in range(2):
        for ref in (keep, give):
            ref[side, 432:448, :] = jnp.zeros((16, 256), F32)

    def store(side, lines, kept, given):
        keep[side, lines, :] = kept + in_keep[side, lines, :]
        give[side, lines, :] = given + in_give[side, lines, :]

    places = [[(rim, 0), (field, 0), (field, 1)], [(field, 2), (field, 3), (rim, 1)]]
    weight_sums(
        at, 2, lambda k, row: grad[3 * k, row], lambda k, a: places[k][a], store, stacked
    )


def input_terms(at, lines, planes, turned, turned_edge, outs, stacked, held):
    half, starts = at[1], starts_of(at[0])
    rows, width = 8, stacked.shape[2] // 3
    for plane, line_of in enumerate(lines):
        for row in range(rows):
            for c, value in enumerate(spread(line_of(row))):
                stacked[plane, row + 1, width * c : width * (c + 1), :] = value
        for row in (0, 9):
            stacked[plane, row] = jnp.zeros(stacked.shape[2:], BF16)

    def store(places):
        for start, ref in zip(starts, outs):
            block = held[pl.ds(start, 64), :]
            for r, (plane, row) in enumerate(places):
                ref[plane, row] = block[:, 128 * r : 128 * r + 128].astype(ref.dtype)

    def step(index, carry):
        row = 2 * index
        for first, plane in planes:
            terms = jnp.concatenate(
                [
                    pair_of(stacked, first + 2 - a, row + 2 - b)
                    for a in range(3)
                    for b in range(3)
                ],
                axis=0,
            )
            held[...] = jnp.dot(turned[...], terms, preferred_element_type=F32)
            store([(plane, row), (plane, row + 1)])
        return carry

    lax.fori_loop(0, rows // 2, step, 0)
    nearest = 8 - 7 * half
    terms = jnp.concatenate(
        [
            jnp.concatenate([stacked[first + 2 - a, nearest] for first, _ in planes], axis=1)
            for a in range(3)
        ],
        axis=0,
    )
    held[...] = jnp.dot(turned_edge[...], terms, preferred_element_type=F32)
    store([(plane, rows) for _, plane in planes])


def inner_input_body(at, grad, turned, turned_edge, after, own, near, far, back, stacked, held):
    lines = [lambda row, k=k: grad[k, row] for k in range(4)]
    input_terms(
        at, lines, [(0, 0), (1, 1)], turned, turned_edge, (own, near, far, back), stacked, held
    )


def outer_input_body(at, grad, low, high, turned, turned_edge, *refs):
    given, outs, (stacked, held) = refs[:4], refs[5:9], refs[9:]
    for source, ref in zip(given, outs):
        for plane in range(2):
            ref[plane + 1] = source[plane]
    lines = [lambda row, k=k: grad[k, row] for k in range(4)]
    lines = [lambda row: low[row]] + lines + [lambda row: high[row]]
    input_terms(at, lines, [(0, 0), (3, 3)], turned, turned_edge, outs, stacked, held)


def total_body(at, own, near, far, back, kept, edges, sent):
    half = at[1]
    mine = pl.multiple_of(32 * half, 32)
    others = pl.multiple_of(32 * (1 - half), 32)

    def sums(plane, row, start):
        value = own[plane, row, pl.ds(start, 32), :]
        for ref in (near, far, back):
            value = value + ref[plane, row, pl.ds(start, 32), :].astype(F32)
        return value

    for plane in range(4):
        for row in range(8):
            kept[plane, row] = sums(plane, row, mine).astype(BF16)
        edges[plane, 0] = sums(plane, 7 * (1 - half), mine)
        edges[plane, 1] = sums(plane, 8, mine)
        for row in range(9):
            sent[plane, row] = sums(plane, row, others).astype(BF16)


def join_body(at, kept, edges, got, after, joined):
    half = at[1]
    for plane in range(4):
        for row in range(8):
            joined[plane, 8 * half + row] = kept[plane, row]
            joined[plane, 8 - 8 * half + row] = got[plane, row]
        joined[plane, 8 * half + 7 * (1 - half)] = (
            edges[plane, 0] + got[plane, 8].astype(F32)
        ).astype(BF16)
        joined[plane, 8 - 8 * half + 7 * half] = (
            edges[plane, 1] + got[plane, 7 * half].astype(F32)
        ).astype(BF16)


def add_body(at, keep, got, first, second, third, chip):
    chip[...] = (keep[...] + got[...]).astype(BF16)


def mean_body(at, pieces, copies):
    total = pieces[0].astype(F32)
    for k in range(1, pieces.shape[0]):
        total = total + pieces[k].astype(F32)
    total = total * (1.0 / math.sqrt(64 * 16 * 128))
    for k in range(copies.shape[0]):
        copies[k] = total


def weave_body(at, mine, other, joined):
    core = at[2]
    for tap in range(27):
        first, second = (ref[16 * tap : 16 * tap + 16] for ref in (mine, other))
        joined[tap, :16] = jnp.where(core == 0, first, second)
        joined[tap, 16:] = jnp.where(core == 0, second, first)


def call(body, n_in, outs, scratch, flops, after=0):
    vmem = pl.BlockSpec(memory_space=pltpu.VMEM)
    anywhere = pl.BlockSpec(memory_space=pl.ANY)
    return pl.pallas_call(
        body,
        out_shape=[jax.ShapeDtypeStruct(*out) for out in outs],
        in_specs=[pl.BlockSpec(memory_space=pltpu.SMEM)]
        + [vmem] * (n_in - 1)
        + [anywhere] * after,
        out_specs=[vmem] * len(outs),
        scratch_shapes=scratch,
        compiler_params=pltpu.CompilerParams(vmem_limit_bytes=VMEM_LIMIT),
        cost_estimate=pl.CostEstimate(
            flops=flops, bytes_accessed=8 * 2**20, transcendentals=2**18
        ),
    )


def on_device(volume, kernel, bias, cotangent):
    here_y, half, core = lax.axis_index("y"), lax.axis_index("xh"), lax.axis_index("core")
    at = jnp.stack([here_y, half, core]).astype(jnp.int32)

    def swap(value):
        return lax.ppermute(value, "xh", [(0, 1), (1, 0)])

    def swap_core(value):
        return lax.ppermute(value, "core", [(0, 1), (1, 0)])

    def turn(value, step):
        return lax.ppermute(value, "y", [(i, (i + step) % 4) for i in range(4)])

    def up(value):
        return lax.ppermute(value, SPACE, [(i, i + 1) for i in range(15)])

    def down(value):
        return lax.ppermute(value, SPACE, [(i + 1, i) for i in range(15)])

    mine = lax.dynamic_slice_in_dim(volume, 7 * half, 9, axis=1)
    theirs = lax.dynamic_slice_in_dim(volume, 7 * (1 - half), 9, axis=1)
    got = swap(theirs)
    own_lo, own_hi = (
        jnp.where(
            half == 0,
            jnp.concatenate([mine[k : k + 2], got[k : k + 2]], axis=2),
            jnp.concatenate([got[k : k + 2], mine[k : k + 2]], axis=2),
        )
        for k in (0, 2)
    )
    left_lo, right_hi = turn(own_lo, 1), turn(own_hi, -1)
    left_hi, right_lo = turn(own_hi, 1), turn(own_lo, -1)
    far_lo, far_hi = turn(left_lo, 1), turn(right_hi, -1)
    kernel_sent, cot_own = call(
        ready_body, 4, [((45, 32, 256), BF16), ((4, 8, 32, 128), BF16)],
        [], 10**6, 1,
    )(at, kernel, jnp.broadcast_to(bias[:, None], (32, 128)), cotangent, theirs)
    kernel_other = swap(kernel_sent)
    up_rim, down_rim = call(rims_body, 9, [((4, 9, 64, 128), BF16)] * 2, [], 10**6, 1)(
        at, own_lo, own_hi, left_lo, left_hi, right_lo, right_hi, far_lo, far_hi,
        kernel_other,
    )
    low, high = up(up_rim), down(down_rim)

    flops = 36 * 10**8
    out_own, out_other, grad, field, taps, bias_wide = call(
        inner_body, 12,
        [
            ((2, 8, 32, 128), BF16), ((2, 8, 32, 128), BF16), ((2, 8, 64, 128), BF16),
            ((4, 10, 256, 128), BF16), ((9, 192, 256), BF16),
            ((64, 128), F32),
        ],
        [], flops // 2,
    )(at, own_lo, own_hi, left_lo, left_hi, right_lo, right_hi, far_lo, far_hi,
      kernel_sent, kernel_other, cot_own)
    keep, give, turned, turned_edge = call(
        inner_weight_body, 4,
        [((2, 448, 256), F32)] * 2 + [((256, 1728), BF16), ((256, 576), BF16)],
        [pltpu.VMEM((2, 8, 192, 128), BF16)], flops // 2,
    )(at, field, grad, taps)
    out_own, out_other, grad, first, last, rim = call(
        outer_body, 11,
        [
            ((4, 8, 32, 128), BF16), ((4, 8, 32, 128), BF16), ((4, 8, 64, 128), BF16),
            ((8, 64, 128), BF16), ((8, 64, 128), BF16), ((2, 10, 256, 128), BF16),
        ],
        [], flops // 2, 1,
    )(at, field, low, high, taps, bias_wide, cot_own, kernel_other,
      out_own, out_other, grad, keep)

    got_out = swap(out_other)
    output = jnp.where(
        half == 0,
        jnp.concatenate([out_own, got_out], axis=1),
        jnp.concatenate([got_out, out_own], axis=1),
    )
    grad_low, grad_high = up(last), down(first)

    def input_chunk(chunk, rim):
        return call(
            functools.partial(input_body, chunk), 5,
            [((2, 9, 64, 128), F32)] + [((2, 9, 64, 128), BF16)] * 3,
            [pltpu.VMEM((4, 10, 192, 128), BF16), pltpu.VMEM((256, 256), F32)],
            flops // 2,
        )(at, grad, rim, turned, turned_edge)

    def input_shapes(planes):
        return [((planes, 9, 64, 128), F32)] + [((planes, 9, 64, 128), BF16)] * 3

    def input_scratch(planes):
        return [pltpu.VMEM((planes, 10, 192, 128), BF16), pltpu.VMEM((256, 256), F32)]

    keep, give = call(
        outer_weight_body, 6, [((2, 448, 256), F32)] * 2,
        [pltpu.VMEM((2, 8, 192, 128), BF16)], flops // 2, 1,
    )(at, field, rim, grad, keep, give, grad)
    parts = call(
        inner_input_body, 4, input_shapes(2), input_scratch(4), flops // 2, 1
    )(at, grad, turned, turned_edge, keep)
    own, near, far, back = call(
        outer_input_body, 10, input_shapes(4), input_scratch(6), flops // 2, 1
    )(at, grad, grad_low, grad_high, turned, turned_edge, *parts, keep)
    (chip,) = call(add_body, 3, [((2, 448, 256), BF16)], [], 10**6, 3)(
        at, keep, swap_core(give), near, near, near
    )
    pieces = lax.all_to_all(
        chip.reshape(16, 56, 256), ("xh", "z", "xl"), 0, 0, tiled=True
    )
    near, back, far = turn(near, 1), turn(back, -1), turn(far, 2)
    kept, edges, sent = call(
        total_body, 5,
        [((4, 8, 32, 128), BF16), ((4, 2, 32, 128), F32), ((4, 9, 32, 128), BF16)], [], 10**6,
    )(at, own, near, far, back)
    got = swap(sent)
    (copies,) = call(mean_body, 2, [((8, 56, 256), F32)], [], 10**6)(at, pieces)
    everyone = lax.all_to_all(copies, ("z", "xl"), 0, 0, tiled=True).reshape(448, 256)
    (weight_grad,) = call(weave_body, 3, [((27, 32, 256), F32)], [], 10**6)(
        at, everyone, swap_core(everyone)
    )
    (input_grad,) = call(join_body, 4, [((4, 16, 32, 128), BF16)], [], 10**6, 1)(
        at, kept, edges, got, weight_grad
    )
    return output, input_grad, weight_grad


def solution(mesh):
    split = Mesh(mesh.devices.reshape(4, 2, 4, 2, 2), CHAN + SPACE)
    return jax.shard_map(
        on_device,
        mesh=split,
        in_specs=(
            P(SPACE, None, CHAN, None),
            P(None, CHAN, None),
            P(CHAN),
            P(SPACE, None, CHAN, None),
        ),
        out_specs=(
            P(SPACE, None, CHAN, None),
            P(SPACE, None, CHAN, None),
            P(None, CHAN, None),
        ),
        check_vma=False,
    )
```

```python
import functools
import math

import jax
import jax.numpy as jnp
from jax import lax
from jax.experimental import pallas as pl
from jax.experimental.pallas import tpu as pltpu
from jax.sharding import Mesh
from jax.sharding import PartitionSpec as P

BF16 = jnp.bfloat16
F32 = jnp.float32
VMEM_LIMIT = 20 * 1024 * 1024
CHAN = ("y", "xh")
SPACE = ("z", "xl", "core")


def moved(value, step):
    if step == 0:
        return value
    size = value.shape[-1]
    lane = lax.broadcasted_iota(jnp.int32, value.shape, value.ndim - 1)
    rolled = pltpu.roll(value, step % size, value.ndim - 1)
    edge = 0 if step == 1 else size - 1
    return jnp.where(lane == edge, 0.0, rolled)


def pair_of(ref, plane, row):
    return jnp.concatenate([ref[plane, row], ref[plane, row + 1]], axis=1)


def starts_of(here_y):
    return [pl.multiple_of(lax.rem(here_y + shift, 4) * 64, 64) for shift in range(4)]


def forward_rows(row, places, kernel, bias, cot_own, cot_other, out_own, out_other, grad,
                 plane_cot, plane_out):
    outs = kernel.shape[1] // 3
    total = jnp.zeros((3 * outs, 256), F32)
    for a, (ref, plane) in enumerate(places):
        for b in range(3):
            total = total + jnp.dot(
                kernel[3 * a + b], pair_of(ref, plane, row + b), preferred_element_type=F32
            )
    others = cot_other[29 + 4 * plane_cot + row // 2]
    for r in range(2):
        part = total[:, 128 * r : 128 * r + 128]
        pre = (
            moved(part[:outs], 1) + part[outs : 2 * outs] + moved(part[2 * outs :], -1)
            + bias[...]
        )
        sig = 1.0 / (1.0 + jnp.exp(-pre))
        out = (pre * sig).astype(BF16)
        out_own[plane_out, row + r] = out[: outs // 2]
        out_other[plane_out, row + r] = out[outs // 2 :]
        cot = jnp.concatenate(
            [cot_own[plane_cot, row + r], others[:, 128 * r : 128 * r + 128]], axis=0
        ).astype(F32)
        grad[plane_out, row + r] = (cot * sig * (1.0 + pre * (1.0 - sig))).astype(BF16)


def ready_body(at, kernel, bias, cotangent, after, kernel_out, cot_own):
    half = at[1]
    kernel_out[:27] = kernel[...]
    rest = bias[...]
    for k in range(3):
        part = rest.astype(BF16)
        kernel_out[27 + k // 2, :, 128 * (k % 2) : 128 * (k % 2) + 128] = part
        rest = rest - part.astype(F32)
    kernel_out[28, :, 128:] = jnp.zeros((32, 128), BF16)
    for plane in range(4):
        for row in range(8):
            cot_own[plane, row] = cotangent[plane, 8 * half + row]
            place, low = 29 + 4 * plane + row // 2, 128 * (row % 2)
            kernel_out[place, :, low : low + 128] = cotangent[plane, 8 - 8 * half + row]


def rims_body(at, own_lo, own_hi, left_lo, left_hi, right_lo, right_hi, far_lo, far_hi,
              kernel, up_rim, down_rim):
    for k, (lower, upper) in enumerate(
        ((own_lo, own_hi), (right_lo, right_hi), (far_lo, far_hi), (left_lo, left_hi))
    ):
        up_rim[k] = upper[1]
        down_rim[k] = lower[0]


def inner_body(at, own_lo, own_hi, left_lo, left_hi, right_lo, right_hi, far_lo, far_hi,
               kernel_own, kernel_other, cot_own, out_own, out_other, grad,
               field, kernel, bias):
    half, starts = at[1], starts_of(at[0])
    rows = own_lo.shape[1]

    def fill_kernel(ab, carry):
        for c in range(3):
            kernel[ab, 64 * c : 64 * c + 32] = kernel_own[3 * ab + c]
            kernel[ab, 64 * c + 32 : 64 * c + 64] = kernel_other[3 * ab + c]
        return carry

    lax.fori_loop(0, 9, fill_kernel, 0)
    for k, ref in enumerate((kernel_own, kernel_other)):
        bias[32 * k : 32 * k + 32] = (
            ref[27, :, :128].astype(F32) + ref[27, :, 128:].astype(F32)
        ) + ref[28, :, :128].astype(F32)
    sources = (own_lo, own_hi), (right_lo, right_hi), (far_lo, far_hi), (left_lo, left_hi)

    def fill(k, carry):
        for upper in range(2):
            plane = k + 2 * upper
            for row in range(rows):
                for start, pair in zip(starts, sources):
                    field[plane, row + 1 - half, pl.ds(start, 64), :] = pair[upper][k, row]
            field[plane, 9 * half] = jnp.zeros(field.shape[2:], BF16)
        return carry

    lax.fori_loop(0, 2, fill, 0)

    def step(index, carry):
        plane, row = index // 4, 2 * lax.rem(index, 4)
        forward_rows(
            row, [(field, plane), (field, plane + 1), (field, plane + 2)], kernel, bias,
            cot_own, kernel_other, out_own, out_other, grad, plane + 1, plane,
        )
        return carry

    lax.fori_loop(0, 8, step, 0)


def outer_body(at, field, low, high, kernel, bias, cot_own, cot_other,
               in_own, in_other, in_grad, after, out_own, out_other, grad, first, last, rim):
    half, starts = at[1], starts_of(at[0])
    for side, ref in ((0, low), (1, high)):
        for row in range(ref.shape[1]):
            for k, start in enumerate(starts):
                rim[side, row + 1 - half, pl.ds(start, 64), :] = ref[k, row]
        rim[side, 9 * half] = jnp.zeros(rim.shape[2:], BF16)
    for plane in range(2):
        out_own[plane + 1] = in_own[plane]
        out_other[plane + 1] = in_other[plane]
        grad[plane + 1] = in_grad[plane]

    def step(index, carry):
        row = 2 * index
        forward_rows(
            row, [(rim, 0), (field, 0), (field, 1)], kernel, bias,
            cot_own, cot_other, out_own, out_other, grad, 0, 0,
        )
        forward_rows(
            row, [(field, 2), (field, 3), (rim, 1)], kernel, bias,
            cot_own, cot_other, out_own, out_other, grad, 3, 3,
        )
        for r in range(2):
            first[row + r] = grad[0, row + r]
            last[row + r] = grad[3, row + r]
        return carry

    lax.fori_loop(0, 4, step, 0)


def spread(line):
    wide = line.astype(F32)
    return [moved(wide, c - 1).astype(BF16) for c in range(3)]


def weight_sums(at, planes, grad_of, cells_of, store, stacked):
    rows, outs = stacked.shape[1], stacked.shape[2] // 3
    for k in range(planes):
        for row in range(rows):
            for c, line in enumerate(spread(grad_of(k, row))):
                stacked[k, row, outs * c : outs * (c + 1), :] = line
    for a in range(3):

        def step(b, carry):
            total = jnp.zeros((256, 3 * outs), F32)
            for k in range(planes):
                grads = jnp.concatenate([stacked[k, row] for row in range(rows)], axis=1)
                ref, plane = cells_of(k, a)
                cells = jnp.concatenate([ref[plane, row + b] for row in range(rows)], axis=1)
                total = total + lax.dot_general(
                    cells, grads, (((1,), (1,)), ((), ())), preferred_element_type=F32
                )
            total = total.T
            for c in range(3):
                line = pl.multiple_of(16 * (9 * a + 3 * b + c), 16)
                for side in range(2):
                    low = outs * c + 32 * side
                    parts = total[low : low + 16], total[low + 16 : low + 32]
                    kept = jnp.where(at[2] == 0, parts[0], parts[1])
                    given = jnp.where(at[2] == 0, parts[1], parts[0])
                    store(side ^ at[1], pl.ds(line, 16), kept, given)
            return carry

        lax.fori_loop(0, 3, step, 0)


def inner_weight_body(at, field, grad, kernel, keep, give, turned, turned_edge, stacked):
    width = kernel.shape[1]
    wide = [kernel[ab] for ab in range(9)]
    for k in range(0, 8, 2):
        turned[:, width * k : width * (k + 2)] = jnp.concatenate(wide[k : k + 2], axis=0).T
    turned[:, 8 * width :] = wide[8].T
    beside = [
        jnp.where(at[1] == 0, kernel[3 * a + 2], kernel[3 * a]) for a in range(3)
    ]
    turned_edge[...] = jnp.concatenate(beside, axis=0).T

    def store(side, lines, kept, given):
        keep[side, lines, :] = kept
        give[side, lines, :] = given

    weight_sums(
        at, 2, lambda k, row: grad[k, row], lambda k, a: (field, k + a), store, stacked
    )


def outer_weight_body(at, field, rim, grad, in_keep, in_give, after, keep, give, stacked):
    for side in range(2):
        for ref in (keep, give):
            ref[side, 432:448, :] = jnp.zeros((16, 256), F32)

    def store(side, lines, kept, given):
        keep[side, lines, :] = kept + in_keep[side, lines, :]
        give[side, lines, :] = given + in_give[side, lines, :]

    places = [[(rim, 0), (field, 0), (field, 1)], [(field, 2), (field, 3), (rim, 1)]]
    weight_sums(
        at, 2, lambda k, row: grad[3 * k, row], lambda k, a: places[k][a], store, stacked
    )


def input_terms(at, lines, planes, place, turned, turned_edge, outs, stacked, held):
    half, starts = at[1], starts_of(at[0])
    rows, width = 8, stacked.shape[2] // 3
    for plane, line_of in enumerate(lines):
        for row in range(rows):
            for c, value in enumerate(spread(line_of(row))):
                stacked[plane, row + 1, width * c : width * (c + 1), :] = value
        for row in (0, 9):
            stacked[plane, row] = jnp.zeros(stacked.shape[2:], BF16)

    def store(places):
        for start, ref in zip(starts, outs):
            block = held[pl.ds(start, 64), :]
            for r, (plane, row) in enumerate(places):
                ref[plane, row] = block[:, 128 * r : 128 * r + 128].astype(ref.dtype)

    def step(index, carry):
        row = 2 * index
        for first, plane in planes:
            terms = jnp.concatenate(
                [
                    pair_of(*place(first + 2 - a), row + 2 - b)
                    for a in range(3)
                    for b in range(3)
                ],
                axis=0,
            )
            held[...] = jnp.dot(turned[...], terms, preferred_element_type=F32)
            store([(plane, row), (plane, row + 1)])
        return carry

    lax.fori_loop(0, rows // 2, step, 0)
    nearest = 8 - 7 * half

    def line_at(plane):
        ref, plane = place(plane)
        return ref[plane, nearest]

    terms = jnp.concatenate(
        [
            jnp.concatenate([line_at(first + 2 - a) for first, _ in planes], axis=1)
            for a in range(3)
        ],
        axis=0,
    )
    held[...] = jnp.dot(turned_edge[...], terms, preferred_element_type=F32)
    store([(plane, rows) for _, plane in planes])


def inner_input_body(at, grad, turned, turned_edge, after, own, near, far, back, stacked, held):
    lines = [lambda row, k=k: grad[k, row] for k in range(4)]
    input_terms(
        at, lines, [(0, 0), (1, 1)], lambda plane: (stacked, plane), turned, turned_edge,
        (own, near, far, back), stacked, held,
    )


def outer_input_body(at, inner, low, high, turned, turned_edge, *refs):
    given, outs, (stacked, held) = refs[:4], refs[5:9], refs[9:]
    for source, ref in zip(given, outs):
        for plane in range(2):
            ref[plane + 1] = source[plane]
    lines = [lambda row: low[row], lambda row: high[row]]

    def place(plane):
        return (inner, plane - 1) if 0 < plane < 5 else (stacked, plane // 5)

    input_terms(at, lines, [(0, 0), (3, 3)], place, turned, turned_edge, outs, stacked, held)


def total_body(at, own, near, far, back, kept, edges, sent):
    half = at[1]
    mine = pl.multiple_of(32 * half, 32)
    others = pl.multiple_of(32 * (1 - half), 32)

    def sums(plane, row, start):
        value = own[plane, row, pl.ds(start, 32), :]
        for ref in (near, far, back):
            value = value + ref[plane, row, pl.ds(start, 32), :].astype(F32)
        return value

    for plane in range(4):
        for row in range(8):
            kept[plane, row] = sums(plane, row, mine).astype(BF16)
        edges[plane, 0] = sums(plane, 7 * (1 - half), mine)
        edges[plane, 1] = sums(plane, 8, mine)
        for row in range(9):
            sent[plane, row] = sums(plane, row, others).astype(BF16)


def join_body(at, kept, edges, got, after, joined):
    half = at[1]
    for plane in range(4):
        for row in range(8):
            joined[plane, 8 * half + row] = kept[plane, row]
            joined[plane, 8 - 8 * half + row] = got[plane, row]
        joined[plane, 8 * half + 7 * (1 - half)] = (
            edges[plane, 0] + got[plane, 8].astype(F32)
        ).astype(BF16)
        joined[plane, 8 - 8 * half + 7 * half] = (
            edges[plane, 1] + got[plane, 7 * half].astype(F32)
        ).astype(BF16)


def add_body(at, keep, got, first, second, third, chip):
    chip[...] = (keep[...] + got[...]).astype(BF16)


def mean_body(at, pieces, copies):
    total = pieces[0].astype(F32)
    for k in range(1, pieces.shape[0]):
        total = total + pieces[k].astype(F32)
    total = total * (1.0 / math.sqrt(64 * 16 * 128))
    for k in range(copies.shape[0]):
        copies[k] = total


def weave_body(at, mine, other, joined):
    core = at[2]
    for tap in range(27):
        first, second = (ref[16 * tap : 16 * tap + 16] for ref in (mine, other))
        joined[tap, :16] = jnp.where(core == 0, first, second)
        joined[tap, 16:] = jnp.where(core == 0, second, first)


def call(body, n_in, outs, scratch, flops, after=0):
    vmem = pl.BlockSpec(memory_space=pltpu.VMEM)
    anywhere = pl.BlockSpec(memory_space=pl.ANY)
    return pl.pallas_call(
        body,
        out_shape=[jax.ShapeDtypeStruct(*out) for out in outs],
        in_specs=[pl.BlockSpec(memory_space=pltpu.SMEM)]
        + [vmem] * (n_in - 1)
        + [anywhere] * after,
        out_specs=[vmem] * len(outs),
        scratch_shapes=scratch,
        compiler_params=pltpu.CompilerParams(vmem_limit_bytes=VMEM_LIMIT),
        cost_estimate=pl.CostEstimate(
            flops=flops, bytes_accessed=8 * 2**20, transcendentals=2**18
        ),
    )


def on_device(volume, kernel, bias, cotangent):
    here_y, half, core = lax.axis_index("y"), lax.axis_index("xh"), lax.axis_index("core")
    at = jnp.stack([here_y, half, core]).astype(jnp.int32)

    def swap(value):
        return lax.ppermute(value, "xh", [(0, 1), (1, 0)])

    def swap_core(value):
        return lax.ppermute(value, "core", [(0, 1), (1, 0)])

    def turn(value, step):
        return lax.ppermute(value, "y", [(i, (i + step) % 4) for i in range(4)])

    def up(value):
        return lax.ppermute(value, SPACE, [(i, i + 1) for i in range(15)])

    def down(value):
        return lax.ppermute(value, SPACE, [(i + 1, i) for i in range(15)])

    mine = lax.dynamic_slice_in_dim(volume, 7 * half, 9, axis=1)
    theirs = lax.dynamic_slice_in_dim(volume, 7 * (1 - half), 9, axis=1)
    got = swap(theirs)
    own_lo, own_hi = (
        jnp.where(
            half == 0,
            jnp.concatenate([mine[k : k + 2], got[k : k + 2]], axis=2),
            jnp.concatenate([got[k : k + 2], mine[k : k + 2]], axis=2),
        )
        for k in (0, 2)
    )
    left_lo, right_hi = turn(own_lo, 1), turn(own_hi, -1)
    left_hi, right_lo = turn(own_hi, 1), turn(own_lo, -1)
    far_lo, far_hi = turn(left_lo, 1), turn(right_hi, -1)
    kernel_sent, cot_own = call(
        ready_body, 4, [((45, 32, 256), BF16), ((4, 8, 32, 128), BF16)],
        [], 10**6, 1,
    )(at, kernel, jnp.broadcast_to(bias[:, None], (32, 128)), cotangent, theirs)
    kernel_other = swap(kernel_sent)
    up_rim, down_rim = call(rims_body, 9, [((4, 9, 64, 128), BF16)] * 2, [], 10**6, 1)(
        at, own_lo, own_hi, left_lo, left_hi, right_lo, right_hi, far_lo, far_hi,
        kernel_other,
    )
    low, high = up(up_rim), down(down_rim)

    flops = 36 * 10**8
    out_own, out_other, grad, field, taps, bias_wide = call(
        inner_body, 12,
        [
            ((2, 8, 32, 128), BF16), ((2, 8, 32, 128), BF16), ((2, 8, 64, 128), BF16),
            ((4, 10, 256, 128), BF16), ((9, 192, 256), BF16),
            ((64, 128), F32),
        ],
        [], flops // 2,
    )(at, own_lo, own_hi, left_lo, left_hi, right_lo, right_hi, far_lo, far_hi,
      kernel_sent, kernel_other, cot_own)
    keep, give, turned, turned_edge = call(
        inner_weight_body, 4,
        [((2, 448, 256), F32)] * 2 + [((256, 1728), BF16), ((256, 576), BF16)],
        [pltpu.VMEM((2, 8, 192, 128), BF16)], flops // 2,
    )(at, field, grad, taps)
    out_own, out_other, grad, first, last, rim = call(
        outer_body, 11,
        [
            ((4, 8, 32, 128), BF16), ((4, 8, 32, 128), BF16), ((4, 8, 64, 128), BF16),
            ((8, 64, 128), BF16), ((8, 64, 128), BF16), ((2, 10, 256, 128), BF16),
        ],
        [], flops // 2, 1,
    )(at, field, low, high, taps, bias_wide, cot_own, kernel_other,
      out_own, out_other, grad, keep)

    got_out = swap(out_other)
    output = jnp.where(
        half == 0,
        jnp.concatenate([out_own, got_out], axis=1),
        jnp.concatenate([got_out, out_own], axis=1),
    )
    grad_low, grad_high = up(last), down(first)

    def input_chunk(chunk, rim):
        return call(
            functools.partial(input_body, chunk), 5,
            [((2, 9, 64, 128), F32)] + [((2, 9, 64, 128), BF16)] * 3,
            [pltpu.VMEM((4, 10, 192, 128), BF16), pltpu.VMEM((256, 256), F32)],
            flops // 2,
        )(at, grad, rim, turned, turned_edge)

    def input_shapes(planes):
        return [((planes, 9, 64, 128), F32)] + [((planes, 9, 64, 128), BF16)] * 3

    def input_scratch(planes):
        lines = [pltpu.VMEM((planes, 10, 192, 128), BF16)] if planes else []
        return lines + [pltpu.VMEM((256, 256), F32)]

    keep, give = call(
        outer_weight_body, 6, [((2, 448, 256), F32)] * 2,
        [pltpu.VMEM((2, 8, 192, 128), BF16)], flops // 2, 1,
    )(at, field, rim, grad, keep, give, grad)
    *parts, lines = call(
        inner_input_body, 4, input_shapes(2) + [((4, 10, 192, 128), BF16)], input_scratch(0), flops // 2, 1
    )(at, grad, turned, turned_edge, keep)
    own, near, far, back = call(
        outer_input_body, 10, input_shapes(4), input_scratch(2), flops // 2, 1
    )(at, lines, grad_low, grad_high, turned, turned_edge, *parts, keep)
    (chip,) = call(add_body, 3, [((2, 448, 256), BF16)], [], 10**6, 3)(
        at, keep, swap_core(give), near, near, near
    )
    pieces = lax.all_to_all(
        chip.reshape(16, 56, 256), ("xh", "z", "xl"), 0, 0, tiled=True
    )
    near, back, far = turn(near, 1), turn(back, -1), turn(far, 2)
    kept, edges, sent = call(
        total_body, 5,
        [((4, 8, 32, 128), BF16), ((4, 2, 32, 128), F32), ((4, 9, 32, 128), BF16)], [], 10**6,
    )(at, own, near, far, back)
    got = swap(sent)
    (copies,) = call(mean_body, 2, [((8, 56, 256), F32)], [], 10**6)(at, pieces)
    everyone = lax.all_to_all(copies, ("z", "xl"), 0, 0, tiled=True).reshape(448, 256)
    (weight_grad,) = call(weave_body, 3, [((27, 32, 256), F32)], [], 10**6)(
        at, everyone, swap_core(everyone)
    )
    (input_grad,) = call(join_body, 4, [((4, 16, 32, 128), BF16)], [], 10**6, 1)(
        at, kept, edges, got, weight_grad
    )
    return output, input_grad, weight_grad


def solution(mesh):
    split = Mesh(mesh.devices.reshape(4, 2, 4, 2, 2), CHAN + SPACE)
    return jax.shard_map(
        on_device,
        mesh=split,
        in_specs=(
            P(SPACE, None, CHAN, None),
            P(None, CHAN, None),
            P(CHAN),
            P(SPACE, None, CHAN, None),
        ),
        out_specs=(
            P(SPACE, None, CHAN, None),
            P(SPACE, None, CHAN, None),
            P(None, CHAN, None),
        ),
        check_vma=False,
    )
```
